128 devices in a mesh: factor: 4 (over z), pair: 32 (over x, y, core).
Axes of the slice: x: 4, y: 4, z: 4, core: 2. Of those that a mesh axis runs over, the one named last changes fastest.
Arguments:
- columns: float32 [16384, 4096], P('factor', 'pair'), parts along dimension 0, may hold values from -250 to 250
- basis: float32 [16384, 4096], P('factor', 'pair'), parts along dimension 0, may hold values from -6 to 6
Outputs:
- new_columns: float32 [16384, 4096], P('factor', 'pair'), parts along dimension 0
- new_basis: float32 [16384, 4096], P('factor', 'pair'), parts along dimension 0
The draws below stay inside these ranges and needn't reach their ends.
There are 4 independent parts, one for each index of `factor`. The reference program is written for one: setup_inputs(seed, part) draws one part's arguments, and reference() takes and returns one part's arrays. A program takes and returns all parts, laid end to end along the dimension named above; each array names one. Nothing has to cross between parts.
All inputs are finite; a program needn't handle non-finite values.
Results may differ from the reference program's by a relative error of at most 0.0014.
Values sent between devices are 32-bit elements; how exact they have to be, the bound alone decides.
A program may use at most 128 MiB of HBM per device.

```python
import math
import jax
import jax.numpy as jnp
import numpy as np
from jax import lax

BS = 64
STEPS = 6
INNER_ROUNDS = 8
N = 4096


def draw_columns(key, part):
    key = jax.random.fold_in(key, 7)
    key_list = jax.random.split(key, 6)
    own_part = jnp.clip(jax.random.normal(key_list[0], (N, N), jnp.float32), -6.0, 6.0)
    low_scale, high_scale = (0.3, 3.0)
    shared_one = jnp.clip(jax.random.normal(key_list[1], (N, 1), jnp.float32), -6.0, 6.0)
    shared_two = jnp.clip(jax.random.normal(key_list[2], (N, 1), jnp.float32), -6.0, 6.0)
    weight_one = jnp.clip(jax.random.normal(key_list[3], (1, N), jnp.float32), -6.0, 6.0)
    weight_two = jnp.clip(jax.random.normal(key_list[4], (1, N), jnp.float32), -6.0, 6.0)
    column_scale = jnp.exp(jax.random.uniform(key_list[5], (1, N), jnp.float32, math.log(low_scale), math.log(high_scale)))
    mixed = own_part + shared_one * weight_one + shared_two * weight_two
    return (column_scale * mixed * (1.0 / math.sqrt(3.0))).astype(jnp.float32)


def block_scale(stream_key, shape, cuts, low, high):
    def one(position, shards_of):
        heights = jax.random.uniform(jax.random.fold_in(jax.random.fold_in(stream_key, 6), position), (shards_of,), jnp.float32, low / len(cuts), high / len(cuts))
        return jnp.repeat(jnp.exp(heights), shape[position] // shards_of).reshape((-1,) + (1,) * (len(shape) - position - 1))

    gain = one(*cuts[0])
    for cut in cuts[1:]:
        gain = gain * one(*cut)
    return gain


def noise(key, dims, width, most, cuts=(), kind=jnp.bfloat16):
    gain = block_scale(key, dims, cuts, -0.22, 0.18) if cuts else 1.0
    values = jax.random.normal(key, dims, jnp.float32) * width * gain
    return jnp.minimum(jnp.maximum(values, -most), most).astype(kind)


def setup_inputs(seed: int = 0, part: int = 0) -> dict:
    seeds = jax.random.split(jax.random.key(seed), 3)
    part_splits = jax.random.split(jax.random.fold_in(seeds[2], part), 3)
    return {
        "columns": draw_columns(jax.random.fold_in(jax.random.fold_in(seeds[2], part), 71), part),
        "basis": noise(part_splits[1], (N, N), 1.0, 6.0, ((1, 32),), jnp.float32),
    }


FULL_PRECISION = lax.Precision.HIGHEST


def pairing(order_width):
    half_width = order_width // 2
    rounds_all = order_width - 1
    left_index = np.zeros((rounds_all, half_width), np.int32)
    right_index = np.zeros((rounds_all, half_width), np.int32)
    for round_no in range(rounds_all):
        ordering = [0] + [1 + (slot_pos - 1 + round_no) % rounds_all for slot_pos in range(1, order_width)]
        for slot_pos in range(half_width):
            left_index[round_no, slot_pos] = ordering[slot_pos]
            right_index[round_no, slot_pos] = ordering[order_width - 1 - slot_pos]
    return left_index, right_index


def rotations(gram_matrix):
    order_width = gram_matrix.shape[-1]
    left_np, right_np = pairing(order_width)
    left_table = jnp.asarray(left_np, dtype=jnp.int32)
    right_table = jnp.asarray(right_np, dtype=jnp.int32)
    positions = jnp.arange(order_width, dtype=jnp.int32)

    def one_round(step_index, carried):
        current, accumulated = carried
        round_row = step_index % (order_width - 1)
        pick_a = (left_table[round_row][:, None] == positions[None, :]).astype(jnp.float32)
        pick_b = (right_table[round_row][:, None] == positions[None, :]).astype(jnp.float32)
        rows_a = jnp.dot(pick_a, current, precision=FULL_PRECISION)
        rows_b = jnp.dot(pick_b, current, precision=FULL_PRECISION)
        diag_a = jnp.sum(rows_a * pick_a, axis=1)
        diag_b = jnp.sum(rows_b * pick_b, axis=1)
        cross_term = jnp.sum(rows_a * pick_b, axis=1)
        spread = diag_a - diag_b
        flip = jnp.where(spread >= 0.0, 1.0, -1.0).astype(jnp.float32)
        half_angle = 0.5 * jnp.arctan2(2.0 * cross_term * flip, jnp.abs(spread))
        cosine = jnp.cos(half_angle)[:, None]
        sine_value = jnp.sin(half_angle)[:, None]
        rotation = jnp.dot(pick_a.T, cosine * pick_a - sine_value * pick_b, precision=FULL_PRECISION)
        rotation = rotation + jnp.dot(pick_b.T, sine_value * pick_a + cosine * pick_b, precision=FULL_PRECISION)
        current = jnp.dot(jnp.dot(rotation.T, current, precision=FULL_PRECISION), rotation, precision=FULL_PRECISION)
        accumulated = jnp.dot(accumulated, rotation, precision=FULL_PRECISION)
        return current, accumulated

    initial = (gram_matrix, jnp.eye(order_width, dtype=jnp.float32))
    return lax.fori_loop(0, INNER_ROUNDS, one_round, initial)[1]


def moved(upper_block, lower_block, axis):
    slot_count = upper_block.shape[axis]
    new_upper = jnp.concatenate([lax.slice_in_dim(upper_block, 0, 1, axis=axis), lax.slice_in_dim(lower_block, 0, 1, axis=axis), lax.slice_in_dim(upper_block, 1, slot_count - 1, axis=axis)], axis=axis)
    new_lower = jnp.concatenate([lax.slice_in_dim(lower_block, 1, slot_count, axis=axis), lax.slice_in_dim(upper_block, slot_count - 1, slot_count, axis=axis)], axis=axis)
    return new_upper, new_lower


def reference(columns, basis):
    order_n = columns.shape[0]
    slot_count = order_n // (2 * BS)
    stacked = jnp.stack([columns, basis]).reshape(2, order_n, slot_count, 2 * BS)
    for step_no in range(STEPS):
        panel = stacked[0]
        gram_all = jnp.einsum("npi,npj->pij", panel, panel, precision=FULL_PRECISION)
        turns = jax.vmap(rotations)(gram_all)
        stacked = jnp.einsum("snpi,pij->snpj", stacked, turns, precision=FULL_PRECISION)
        new_upper, new_lower = moved(stacked[:, :, :, :BS], stacked[:, :, :, BS:], 2)
        stacked = jnp.concatenate([new_upper, new_lower], axis=3)
    final = stacked.reshape(2, order_n, order_n)
    return final[0], final[1]
```

```python
import functools

import jax
import jax.numpy as jnp
from jax import lax
from jax.experimental import pallas as pl
from jax.experimental.pallas import tpu as pltpu
from jax.sharding import PartitionSpec as P

STEPS = 6
INNER_ROUNDS = 8
MESH = pl.DeviceIdType.MESH
F32 = jnp.float32
BF16 = jnp.bfloat16
WIDTH = 128
HALF = 64
ROWS = 512


def iota(shape, dim):
    return lax.broadcasted_iota(jnp.int32, shape, dim)


def partner_of(place, round_no):
    cycle = WIDTH - 1
    j = round_no % cycle
    mirror = 1 + lax.rem(cycle - 2 + 2 * j + 2 * cycle - (place - 1), cycle)
    lone = 1 + (cycle - 1 + j) % cycle
    return jnp.where(place == 0, lone, jnp.where(place == lone, 0, mirror))


def role_of(place, round_no):
    cycle = WIDTH - 1
    j = round_no % cycle
    position = 1 + lax.rem(place - 1 - j + 2 * cycle, cycle)
    return (place == 0) | (position < HALF)


def pick_lanes(value, index):
    return jnp.take_along_axis(value, index, axis=1)


def rsqrt(value):
    guess = lax.rsqrt(value)
    return guess * (1.5 - 0.5 * value * guess * guess)


def angles(diag, cross, partner, first):
    other = pick_lanes(diag, partner)
    spread = jnp.where(first, diag - other, other - diag)
    flip = jnp.where(spread >= 0.0, 1.0, -1.0)
    size = jnp.abs(spread)
    twice = 2.0 * cross * flip
    most = jnp.maximum(size, jnp.abs(twice))
    still = most == 0.0
    most = jnp.where(still, 1.0, most)
    size = jnp.where(still, 1.0, size / most)
    twice = twice / most
    inverse = rsqrt(size * size + twice * twice)
    cos_sq = 0.5 + 0.5 * size * inverse
    inverse_cos = rsqrt(cos_sq)
    cosine = cos_sq * inverse_cos
    sine = 0.5 * twice * inverse * inverse_cos
    return cosine, jnp.where(first, sine, -sine)


def rotations(gram):
    rows = iota((WIDTH, WIDTH), 0)
    lanes = iota((WIDTH, WIDTH), 1)
    few = iota((8, WIDTH), 1)
    current = gram
    accumulated = jnp.where(rows == lanes, 1.0, 0.0).astype(F32)
    for round_no in range(INNER_ROUNDS):
        partner = partner_of(lanes, round_no)
        diag = jnp.sum(jnp.where(rows == lanes, current, 0.0), axis=0, keepdims=True)
        cross = jnp.sum(jnp.where(rows == partner, current, 0.0), axis=0, keepdims=True)
        diag = jnp.broadcast_to(diag, (8, WIDTH))
        cross = jnp.broadcast_to(cross, (8, WIDTH))
        cosine, sine = angles(
            diag, cross, partner_of(few, round_no), role_of(few, round_no)
        )
        cosine = jnp.broadcast_to(cosine[:1], (WIDTH, WIDTH))
        sine = jnp.broadcast_to(sine[:1], (WIDTH, WIDTH))
        turn = lambda m: m * cosine + pick_lanes(m, partner) * sine
        accumulated = turn(accumulated)
        if round_no + 1 < INNER_ROUNDS:
            current = turn(turn(current).T)
    return accumulated


def swap_halves(value):
    return pltpu.roll(value, HALF, 1)


def split(value, parts):
    out = []
    for _ in range(parts - 1):
        part = value.astype(BF16)
        out.append(part)
        value = value - part.astype(F32)
    out.append(value.astype(BF16))
    return out


def folded(big):
    low = iota((HALF, WIDTH), 1) < HALF
    halves = []
    for at in (0, WIDTH):
        one, two = big[at:at + HALF], big[at + HALF:at + WIDTH]
        left = one[:, :WIDTH] + swap_halves(two[:, :WIDTH])
        right = swap_halves(one[:, WIDTH:]) + two[:, WIDTH:]
        halves.append(jnp.where(low, left, right))
    return jnp.concatenate(halves, axis=0)


def expanded(turn, is_first):
    low = iota((HALF, WIDTH), 1) < HALF
    out = []
    for at in (0, HALF):
        rows = turn[at:at + HALF]
        moved = swap_halves(rows)
        for keep in (low, ~low):
            to_upper = jnp.where(keep, rows if keep is low else moved, 0.0)
            to_lower = jnp.where(keep, moved if keep is low else rows, 0.0)
            one = jnp.where(is_first, to_lower, to_upper)
            two = jnp.where(is_first, to_upper, to_lower)
            out.append(jnp.concatenate([one, two], axis=1))
    return jnp.concatenate(out, axis=0)


def kernel(
    slots, x_in, v_in, x_out, v_out,
    panels, staged, gram_sum, turn_parts, load_sem, store_sem, send_sem, recv_sem,
):
    packed = panels.shape[2]
    me = lax.axis_index("pair")
    factor = lax.axis_index("factor")
    right = lax.rem(me + 1, slots)
    left = lax.rem(me + slots - 1, slots)
    is_first = 1 - (me + slots - 1) // slots
    is_last = (me + 1) // slots

    loads = []
    for which, source in enumerate((x_in, v_in)):
        load = pltpu.make_async_copy(source, staged.at[which], load_sem.at[which])
        load.start()
        loads.append(load)

    barrier = pltpu.get_barrier_semaphore()
    for neighbour in (left, right):
        pl.semaphore_signal(
            barrier, inc=1, device_id=(factor, neighbour), device_id_type=MESH
        )
    pl.semaphore_wait(barrier, 2)

    def place(step, side):
        return 2 * step + side

    def rows_of(chunk):
        return pl.ds(pl.multiple_of(chunk * ROWS, ROWS), ROWS)

    def remote(which, step, chunk, side, device):
        return pltpu.make_async_remote_copy(
            src_ref=panels.at[which, place(step, side), rows_of(chunk)],
            dst_ref=panels.at[which, place(step + 1, side), rows_of(chunk)],
            send_sem=send_sem.at[which, place(step, side), chunk],
            recv_sem=recv_sem.at[which, place(step, side), chunk],
            device_id=(factor, device),
            device_id_type=MESH,
        )

    def to_right(which, step, chunk):
        return remote(which, step, chunk, 0, right)

    def to_left(which, step, chunk):
        return remote(which, step, chunk, 1, left)

    def send(which, step, chunk):
        @pl.when(me < slots - 1)
        def _():
            to_right(which, step, chunk).start()

        @pl.when(me > 0)
        def _():
            to_left(which, step, chunk).start()

    def wait_sent(which, step, chunk):
        @pl.when(me < slots - 1)
        def _():
            to_right(which, step, chunk).wait_send()

        @pl.when(me > 0)
        def _():
            to_left(which, step, chunk).wait_send()

    def wait_received(which, step, chunk):
        @pl.when(me > 0)
        def _():
            to_right(which, step, chunk).wait_recv()

        @pl.when(me < slots - 1)
        def _():
            to_left(which, step, chunk).wait_recv()

    def every_chunk(act):
        def body(chunk, _):
            act(chunk)
            return 0

        lax.fori_loop(0, packed // ROWS, body, 0)

    def pack(which):
        low = iota((ROWS, WIDTH), 1) < HALF

        def body(chunk, _):
            at = pl.ds(pl.multiple_of(chunk * ROWS, ROWS), ROWS)
            other = pl.ds(
                pl.multiple_of(packed + chunk * ROWS, ROWS), ROWS
            )
            one, two = staged[which, at], staged[which, other]
            panels[which, 0, at] = jnp.where(low, one, swap_halves(two))
            panels[which, 1, at] = jnp.where(low, swap_halves(one), two)
            return 0

        lax.fori_loop(0, packed // ROWS, body, 0)

    def unpack(which):
        low = iota((ROWS, WIDTH), 1) < HALF

        def body(chunk, _):
            at = pl.ds(pl.multiple_of(chunk * ROWS, ROWS), ROWS)
            other = pl.ds(
                pl.multiple_of(packed + chunk * ROWS, ROWS), ROWS
            )
            upper = panels[which, place(STEPS, 0), at]
            lower = panels[which, place(STEPS, 1), at]
            staged[which, at] = jnp.where(low, upper, swap_halves(lower))
            staged[which, other] = jnp.where(low, swap_halves(upper), lower)
            return 0

        lax.fori_loop(0, packed // ROWS, body, 0)

    def panel_rows(which, step, at):
        return jnp.concatenate(
            [panels[which, place(step, 0), at], panels[which, place(step, 1), at]], axis=1
        )

    def gram(step):
        gram_sum[...] = jnp.zeros_like(gram_sum)
        inner = lambda a, b: lax.dot_general(
            a, b, (((0,), (0,)), ((), ())), preferred_element_type=F32
        )

        def add(chunk):
            @pl.when(step > 0)
            def _():
                wait_received(0, step - 1, chunk)

            high, low = split(panel_rows(0, step, rows_of(chunk)), 2)
            gram_sum[0] += inner(high, high) + inner(low, low)
            gram_sum[1] += inner(high, low)

        every_chunk(add)
        mixed = gram_sum[1]
        return folded(gram_sum[0] + (mixed + mixed.T))

    def apply(which, step, chunk, terms):
        at = rows_of(chunk)
        high, low = split(panel_rows(which, step, at), 2)
        total = jnp.dot(high, turn_parts[0], preferred_element_type=F32)
        small = jnp.dot(low, turn_parts[0], preferred_element_type=F32)
        for term in range(1, terms):
            small += jnp.dot(high, turn_parts[term], preferred_element_type=F32)
        total += small
        panels[which, place(step, 0) + 3 * is_last, at] = total[:, :WIDTH]
        panels[which, place(step, 1) + is_first, at] = total[:, WIDTH:]

    loads[0].wait()
    pack(0)

    def one_step(step, _):
        sums = gram(step)

        @pl.when(step > 0)
        def _():
            every_chunk(lambda chunk: send(1, step - 1, chunk))

        turn = rotations(sums)
        for term, part in enumerate(split(expanded(turn, is_first == 1), 3)):
            turn_parts[term] = part

        def turn_columns(chunk):
            apply(0, step, chunk, 3)
            send(0, step, chunk)

        every_chunk(turn_columns)

        @pl.when(step == 0)
        def _():
            loads[1].wait()
            pack(1)

        def turn_basis(chunk):
            @pl.when(step > 0)
            def _():
                wait_received(1, step - 1, chunk)

            apply(1, step, chunk, 2)

        every_chunk(turn_basis)
        return 0

    lax.fori_loop(0, STEPS, one_step, 0)
    every_chunk(lambda chunk: wait_received(0, STEPS - 1, chunk))
    every_chunk(lambda chunk: send(1, STEPS - 1, chunk))

    stores = []
    for which, target in enumerate((x_out, v_out)):
        if which:
            every_chunk(lambda chunk: wait_received(1, STEPS - 1, chunk))
        unpack(which)
        store = pltpu.make_async_copy(staged.at[which], target, store_sem.at[which])
        store.start()
        stores.append(store)

    def settle(step, _):
        for which in range(2):
            every_chunk(lambda chunk: wait_sent(which, step, chunk))
        return 0

    lax.fori_loop(0, STEPS, settle, 0)
    for store in stores:
        store.wait()


def on_device(columns, basis):
    rows, width = columns.shape
    slots = lax.axis_size("pair")
    packed = rows // 2
    shape = jax.ShapeDtypeStruct((rows, width), F32)
    return pl.pallas_call(
        functools.partial(kernel, slots),
        out_shape=(shape, shape),
        in_specs=[pl.BlockSpec(memory_space=pl.ANY)] * 2,
        out_specs=(pl.BlockSpec(memory_space=pl.ANY),) * 2,
        scratch_shapes=[
            pltpu.VMEM((2, 2 * STEPS + 2, packed, width), F32),
            pltpu.VMEM((2, rows, width), F32),
            pltpu.VMEM((2, 2 * width, 2 * width), F32),
            pltpu.VMEM((3, 2 * width, 2 * width), BF16),
            pltpu.SemaphoreType.DMA((2,)),
            pltpu.SemaphoreType.DMA((2,)),
            pltpu.SemaphoreType.DMA((2, 2 * STEPS, packed // ROWS)),
            pltpu.SemaphoreType.DMA((2, 2 * STEPS, packed // ROWS)),
        ],
        compiler_params=pltpu.CompilerParams(
            collective_id=0, has_side_effects=True, vmem_limit_bytes=50 * 2**20
        ),
        cost_estimate=pl.CostEstimate(
            flops=6 * 9 * 2 * rows * width * width,
            bytes_accessed=4 * rows * width * 4,
            transcendentals=0,
        ),
    )(columns, basis)


def solution(mesh):
    spec = P("factor", "pair")
    return jax.shard_map(
        on_device, mesh=mesh, in_specs=(spec, spec), out_specs=(spec, spec), check_vma=False
    )
```

```python
import functools

import jax
import jax.numpy as jnp
from jax import lax
from jax.experimental import pallas as pl
from jax.experimental.pallas import tpu as pltpu
from jax.sharding import PartitionSpec as P

STEPS = 6
INNER_ROUNDS = 8
MESH = pl.DeviceIdType.MESH
F32 = jnp.float32
BF16 = jnp.bfloat16
WIDTH = 128
HALF = 64
GRAM_ROWS = 512
APPLY_ROWS = 512


def iota(shape, dim):
    return lax.broadcasted_iota(jnp.int32, shape, dim)


def rsqrt(value):
    guess = lax.rsqrt(value)
    return guess * (1.5 - 0.5 * value * guess * guess)


def sublane_roll(value, shift):
    return pltpu.roll(value, shift % 8, 0)


def order_of(row, shift):
    inside = lax.rem(row, HALF)
    k = 8 * lax.rem(inside, 8) + inside // 8
    k = jnp.where(row < HALF, k, WIDTH - 1 - k)
    return jnp.where(k == 0, 0, 1 + lax.rem(k - 1 + shift, WIDTH - 1))


def order_matrix(shift):
    rows = iota((WIDTH, WIDTH), 0)
    lanes = iota((WIDTH, WIDTH), 1)
    return jnp.where(order_of(rows, shift) == lanes, 1.0, 0.0).astype(F32)


def moved_on(first, second):
    top = iota((8, first.shape[1]), 0) == 0
    end = iota((8, first.shape[1]), 0) == 7
    a, b = first, second
    new_first = jnp.concatenate(
        [
            jnp.where(top, a[:8], a[8:16]),
            a[16:],
            jnp.where(end, b[HALF - 8:], sublane_roll(a[:8], -1)),
        ],
        axis=0,
    )
    new_second = jnp.concatenate(
        [jnp.where(top, a[8:16], sublane_roll(b[HALF - 8:], 1)), b[:HALF - 8]], axis=0
    )
    return new_first, new_second


def angles(diag_a, diag_b, cross):
    spread = diag_a - diag_b
    twice = 2.0 * cross
    twice = jnp.where(spread >= 0.0, twice, -twice)
    size = jnp.abs(spread)
    most = jnp.maximum(size, jnp.abs(twice))
    still = most == 0.0
    scale = pl.reciprocal(jnp.where(still, 1.0, most), approx=True)
    size = jnp.where(still, 1.0, size * scale)
    twice = twice * scale
    inverse = rsqrt(size * size + twice * twice)
    cos_sq = 0.5 + 0.5 * size * inverse
    inverse_cos = rsqrt(cos_sq)
    return cos_sq * inverse_cos, 0.5 * twice * inverse * inverse_cos


def lane_sum(value):
    return jnp.broadcast_to(jnp.sum(value, axis=1, keepdims=True), value.shape)


def rotations(gram):
    start = order_matrix(0)
    start_bf16 = start.astype(BF16)
    pieces = [jnp.dot(start_bf16, part, preferred_element_type=F32) for part in split(gram, 3)]
    ordered = (pieces[0] + pieces[1]) + pieces[2]
    turn_a, turn_b = start[:HALF], start[HALF:]
    with_a, with_b = ordered[:HALF], ordered[HALF:]
    diag_a, diag_b = lane_sum(turn_a * with_a), lane_sum(turn_b * with_b)
    for round_no in range(INNER_ROUNDS):
        cross = lane_sum(turn_a * with_b)
        cosine, sine = angles(diag_a, diag_b, cross)
        turn_a, turn_b = cosine * turn_a + sine * turn_b, cosine * turn_b - sine * turn_a
        if round_no + 1 < INNER_ROUNDS:
            with_a, with_b = cosine * with_a + sine * with_b, cosine * with_b - sine * with_a
            both = 2.0 * cosine * sine * cross
            cos_sq, sin_sq = cosine * cosine, sine * sine
            diag_a, diag_b = (
                cos_sq * diag_a + sin_sq * diag_b + both,
                cos_sq * diag_b + sin_sq * diag_a - both,
            )
            turn_a, turn_b = moved_on(turn_a, turn_b)
            with_a, with_b = moved_on(with_a, with_b)
            diag_a, diag_b = moved_on(diag_a, diag_b)
    end = order_matrix(INNER_ROUNDS - 1).astype(BF16)
    turn = jnp.concatenate([turn_a, turn_b], axis=0)
    pieces = [
        lax.dot_general(part, end, (((0,), (0,)), ((), ())), preferred_element_type=F32)
        for part in split(turn, 3)
    ]
    return (pieces[0] + pieces[1]) + pieces[2]


def swap_halves(value):
    return pltpu.roll(value, HALF, 1)


def split(value, parts):
    out = []
    for _ in range(parts - 1):
        part = value.astype(BF16)
        out.append(part)
        value = value - part.astype(F32)
    out.append(value.astype(BF16))
    return out


def folded(big):
    low = iota((HALF, WIDTH), 1) < HALF
    halves = []
    for at in (0, WIDTH):
        one, two = big[at:at + HALF], big[at + HALF:at + WIDTH]
        left = one[:, :WIDTH] + swap_halves(two[:, :WIDTH])
        right = swap_halves(one[:, WIDTH:]) + two[:, WIDTH:]
        halves.append(jnp.where(low, left, right))
    return jnp.concatenate(halves, axis=0)


def expanded(turn, is_first):
    low = iota((HALF, WIDTH), 1) < HALF
    out = []
    for at in (0, HALF):
        rows = turn[at:at + HALF]
        moved = swap_halves(rows)
        for keep in (low, ~low):
            to_upper = jnp.where(keep, rows if keep is low else moved, 0.0)
            to_lower = jnp.where(keep, moved if keep is low else rows, 0.0)
            one = jnp.where(is_first, to_lower, to_upper)
            two = jnp.where(is_first, to_upper, to_lower)
            out.append(jnp.concatenate([one, two], axis=1))
    return jnp.concatenate(out, axis=0)


def kernel(
    slots, x_in, v_in, x_out, v_out,
    panels, staged, gram_sum, turn_parts, load_sem, store_sem, send_sem, recv_sem,
):
    packed = panels.shape[2]
    me = lax.axis_index("pair")
    factor = lax.axis_index("factor")
    right = lax.rem(me + 1, slots)
    left = lax.rem(me + slots - 1, slots)
    is_first = 1 - (me + slots - 1) // slots
    is_last = (me + 1) // slots

    loads = []
    for which, source in enumerate((x_in, v_in)):
        load = pltpu.make_async_copy(source, staged.at[which], load_sem.at[which])
        load.start()
        loads.append(load)

    barrier = pltpu.get_barrier_semaphore()
    for neighbour in (left, right):
        pl.semaphore_signal(
            barrier, inc=1, device_id=(factor, neighbour), device_id_type=MESH
        )
    pl.semaphore_wait(barrier, 2)

    def place(step, side):
        return 2 * step + side

    def to_right(which, step):
        return pltpu.make_async_remote_copy(
            src_ref=panels.at[which, place(step, 0)],
            dst_ref=panels.at[which, place(step + 1, 0)],
            send_sem=send_sem.at[which, place(step, 0)],
            recv_sem=recv_sem.at[which, place(step, 0)],
            device_id=(factor, right),
            device_id_type=MESH,
        )

    def to_left(which, step):
        return pltpu.make_async_remote_copy(
            src_ref=panels.at[which, place(step, 1)],
            dst_ref=panels.at[which, place(step + 1, 1)],
            send_sem=send_sem.at[which, place(step, 1)],
            recv_sem=recv_sem.at[which, place(step, 1)],
            device_id=(factor, left),
            device_id_type=MESH,
        )

    def send(which, step):
        @pl.when(me < slots - 1)
        def _():
            to_right(which, step).start()

        @pl.when(me > 0)
        def _():
            to_left(which, step).start()

    def wait_sent(which, step):
        @pl.when(me < slots - 1)
        def _():
            to_right(which, step).wait_send()

        @pl.when(me > 0)
        def _():
            to_left(which, step).wait_send()

    def wait_received(which, step):
        @pl.when(me > 0)
        def _():
            to_right(which, step).wait_recv()

        @pl.when(me < slots - 1)
        def _():
            to_left(which, step).wait_recv()

    def pack(which):
        low = iota((APPLY_ROWS, WIDTH), 1) < HALF

        def body(chunk, _):
            at = pl.ds(pl.multiple_of(chunk * APPLY_ROWS, APPLY_ROWS), APPLY_ROWS)
            other = pl.ds(
                pl.multiple_of(packed + chunk * APPLY_ROWS, APPLY_ROWS), APPLY_ROWS
            )
            one, two = staged[which, at], staged[which, other]
            panels[which, 0, at] = jnp.where(low, one, swap_halves(two))
            panels[which, 1, at] = jnp.where(low, swap_halves(one), two)
            return 0

        lax.fori_loop(0, packed // APPLY_ROWS, body, 0)

    def unpack(which):
        low = iota((APPLY_ROWS, WIDTH), 1) < HALF

        def body(chunk, _):
            at = pl.ds(pl.multiple_of(chunk * APPLY_ROWS, APPLY_ROWS), APPLY_ROWS)
            other = pl.ds(
                pl.multiple_of(packed + chunk * APPLY_ROWS, APPLY_ROWS), APPLY_ROWS
            )
            upper = panels[which, place(STEPS, 0), at]
            lower = panels[which, place(STEPS, 1), at]
            staged[which, at] = jnp.where(low, upper, swap_halves(lower))
            staged[which, other] = jnp.where(low, swap_halves(upper), lower)
            return 0

        lax.fori_loop(0, packed // APPLY_ROWS, body, 0)

    def panel_rows(which, step, at):
        return jnp.concatenate(
            [panels[which, place(step, 0), at], panels[which, place(step, 1), at]], axis=1
        )

    def gram(step):
        gram_sum[...] = jnp.zeros_like(gram_sum)
        inner = lambda a, b: lax.dot_general(
            a, b, (((0,), (0,)), ((), ())), preferred_element_type=F32
        )

        def body(chunk, _):
            at = pl.ds(pl.multiple_of(chunk * GRAM_ROWS, GRAM_ROWS), GRAM_ROWS)
            high, low = split(panel_rows(0, step, at), 2)
            gram_sum[0] += inner(high, high) + inner(low, low)
            gram_sum[1] += inner(high, low)
            return 0

        lax.fori_loop(0, packed // GRAM_ROWS, body, 0)
        mixed = gram_sum[1]
        return folded(gram_sum[0] + (mixed + mixed.T))

    def apply(which, step, terms):
        first_place = place(step, 0) + 3 * is_last
        second_place = place(step, 1) + is_first

        def body(chunk, _):
            at = pl.ds(pl.multiple_of(chunk * APPLY_ROWS, APPLY_ROWS), APPLY_ROWS)
            high, low = split(panel_rows(which, step, at), 2)
            total = jnp.dot(high, turn_parts[0], preferred_element_type=F32)
            small = jnp.dot(low, turn_parts[0], preferred_element_type=F32)
            for term in range(1, terms):
                small += jnp.dot(high, turn_parts[term], preferred_element_type=F32)
            total += small
            panels[which, first_place, at] = total[:, :WIDTH]
            panels[which, second_place, at] = total[:, WIDTH:]
            return 0

        lax.fori_loop(0, packed // APPLY_ROWS, body, 0)

    loads[0].wait()
    pack(0)

    def one_step(step, _):
        @pl.when(step > 0)
        def _():
            wait_received(0, step - 1)

        turn = rotations(gram(step))
        for term, part in enumerate(split(expanded(turn, is_first == 1), 3)):
            turn_parts[term] = part
        apply(0, step, 3)
        send(0, step)

        @pl.when(step == 0)
        def _():
            loads[1].wait()
            pack(1)

        @pl.when(step > 0)
        def _():
            wait_received(1, step - 1)

        apply(1, step, 2)
        send(1, step)
        return 0

    lax.fori_loop(0, STEPS, one_step, 0)

    stores = []
    for which, target in enumerate((x_out, v_out)):
        wait_received(which, STEPS - 1)
        unpack(which)
        store = pltpu.make_async_copy(staged.at[which], target, store_sem.at[which])
        store.start()
        stores.append(store)

    def settle(step, _):
        for which in range(2):
            wait_sent(which, step)
        return 0

    lax.fori_loop(0, STEPS, settle, 0)
    for store in stores:
        store.wait()


def on_device(columns, basis):
    rows, width = columns.shape
    slots = lax.axis_size("pair")
    packed = rows // 2
    shape = jax.ShapeDtypeStruct((rows, width), F32)
    return pl.pallas_call(
        functools.partial(kernel, slots),
        out_shape=(shape, shape),
        in_specs=[pl.BlockSpec(memory_space=pl.ANY)] * 2,
        out_specs=(pl.BlockSpec(memory_space=pl.ANY),) * 2,
        scratch_shapes=[
            pltpu.VMEM((2, 2 * STEPS + 2, packed, width), F32),
            pltpu.VMEM((2, rows, width), F32),
            pltpu.VMEM((2, 2 * width, 2 * width), F32),
            pltpu.VMEM((3, 2 * width, 2 * width), BF16),
            pltpu.SemaphoreType.DMA((2,)),
            pltpu.SemaphoreType.DMA((2,)),
            pltpu.SemaphoreType.DMA((2, 2 * STEPS)),
            pltpu.SemaphoreType.DMA((2, 2 * STEPS)),
        ],
        compiler_params=pltpu.CompilerParams(
            collective_id=0, has_side_effects=True, vmem_limit_bytes=50 * 2**20
        ),
        cost_estimate=pl.CostEstimate(
            flops=6 * 9 * 2 * rows * width * width,
            bytes_accessed=4 * rows * width * 4,
            transcendentals=0,
        ),
    )(columns, basis)


def solution(mesh):
    spec = P("factor", "pair")
    return jax.shard_map(
        on_device, mesh=mesh, in_specs=(spec, spec), out_specs=(spec, spec), check_vma=False
    )
```

```python
import functools

import jax
import jax.numpy as jnp
from jax import lax
from jax.experimental import pallas as pl
from jax.experimental.pallas import tpu as pltpu
from jax.sharding import PartitionSpec as P

STEPS = 6
INNER_ROUNDS = 8
MESH = pl.DeviceIdType.MESH
F32 = jnp.float32
BF16 = jnp.bfloat16
WIDTH = 128
HALF = 64
ROWS = 512


def iota(shape, dim):
    return lax.broadcasted_iota(jnp.int32, shape, dim)


def rsqrt(value):
    guess = lax.rsqrt(value)
    return guess * (1.5 - 0.5 * value * guess * guess)


def sublane_roll(value, shift):
    return pltpu.roll(value, shift % 8, 0)


def order_of(row, shift):
    inside = lax.rem(row, HALF)
    k = 8 * lax.rem(inside, 8) + inside // 8
    k = jnp.where(row < HALF, k, WIDTH - 1 - k)
    return jnp.where(k == 0, 0, 1 + lax.rem(k - 1 + shift, WIDTH - 1))


def order_matrix(shift):
    rows = iota((WIDTH, WIDTH), 0)
    lanes = iota((WIDTH, WIDTH), 1)
    return jnp.where(order_of(rows, shift) == lanes, 1.0, 0.0).astype(F32)


def moved_on(first, second):
    top = iota((8, first.shape[1]), 0) == 0
    end = iota((8, first.shape[1]), 0) == 7
    a, b = first, second
    new_first = jnp.concatenate(
        [
            jnp.where(top, a[:8], a[8:16]),
            a[16:],
            jnp.where(end, b[HALF - 8:], sublane_roll(a[:8], -1)),
        ],
        axis=0,
    )
    new_second = jnp.concatenate(
        [jnp.where(top, a[8:16], sublane_roll(b[HALF - 8:], 1)), b[:HALF - 8]], axis=0
    )
    return new_first, new_second


def angles(diag_a, diag_b, cross):
    spread = diag_a - diag_b
    twice = 2.0 * cross
    twice = jnp.where(spread >= 0.0, twice, -twice)
    size = jnp.abs(spread)
    most = jnp.maximum(size, jnp.abs(twice))
    still = most == 0.0
    scale = pl.reciprocal(jnp.where(still, 1.0, most), approx=True)
    size = jnp.where(still, 1.0, size * scale)
    twice = twice * scale
    inverse = rsqrt(size * size + twice * twice)
    cos_sq = 0.5 + 0.5 * size * inverse
    inverse_cos = rsqrt(cos_sq)
    return cos_sq * inverse_cos, 0.5 * twice * inverse * inverse_cos


def lane_sum(value):
    return jnp.broadcast_to(jnp.sum(value, axis=1, keepdims=True), value.shape)


def rotations(gram):
    start = order_matrix(0)
    start_bf16 = start.astype(BF16)
    pieces = [jnp.dot(start_bf16, part, preferred_element_type=F32) for part in split(gram, 3)]
    ordered = (pieces[0] + pieces[1]) + pieces[2]
    turn_a, turn_b = start[:HALF], start[HALF:]
    with_a, with_b = ordered[:HALF], ordered[HALF:]
    diag_a, diag_b = lane_sum(turn_a * with_a), lane_sum(turn_b * with_b)
    for round_no in range(INNER_ROUNDS):
        cross = lane_sum(turn_a * with_b)
        cosine, sine = angles(diag_a, diag_b, cross)
        turn_a, turn_b = cosine * turn_a + sine * turn_b, cosine * turn_b - sine * turn_a
        if round_no + 1 < INNER_ROUNDS:
            with_a, with_b = cosine * with_a + sine * with_b, cosine * with_b - sine * with_a
            both = 2.0 * cosine * sine * cross
            cos_sq, sin_sq = cosine * cosine, sine * sine
            diag_a, diag_b = (
                cos_sq * diag_a + sin_sq * diag_b + both,
                cos_sq * diag_b + sin_sq * diag_a - both,
            )
            turn_a, turn_b = moved_on(turn_a, turn_b)
            with_a, with_b = moved_on(with_a, with_b)
            diag_a, diag_b = moved_on(diag_a, diag_b)
    end = order_matrix(INNER_ROUNDS - 1).astype(BF16)
    turn = jnp.concatenate([turn_a, turn_b], axis=0)
    pieces = [
        lax.dot_general(part, end, (((0,), (0,)), ((), ())), preferred_element_type=F32)
        for part in split(turn, 3)
    ]
    return (pieces[0] + pieces[1]) + pieces[2]


def swap_halves(value):
    return pltpu.roll(value, HALF, 1)


def split(value, parts):
    out = []
    for _ in range(parts - 1):
        part = value.astype(BF16)
        out.append(part)
        value = value - part.astype(F32)
    out.append(value.astype(BF16))
    return out


def folded(big):
    low = iota((HALF, WIDTH), 1) < HALF
    halves = []
    for at in (0, WIDTH):
        one, two = big[at:at + HALF], big[at + HALF:at + WIDTH]
        left = one[:, :WIDTH] + swap_halves(two[:, :WIDTH])
        right = swap_halves(one[:, WIDTH:]) + two[:, WIDTH:]
        halves.append(jnp.where(low, left, right))
    return jnp.concatenate(halves, axis=0)


def expanded(turn, is_first):
    low = iota((HALF, WIDTH), 1) < HALF
    out = []
    for at in (0, HALF):
        rows = turn[at:at + HALF]
        moved = swap_halves(rows)
        for keep in (low, ~low):
            to_upper = jnp.where(keep, rows if keep is low else moved, 0.0)
            to_lower = jnp.where(keep, moved if keep is low else rows, 0.0)
            one = jnp.where(is_first, to_lower, to_upper)
            two = jnp.where(is_first, to_upper, to_lower)
            out.append(jnp.concatenate([one, two], axis=1))
    return jnp.concatenate(out, axis=0)


def kernel(
    slots, x_in, v_in, x_out, v_out,
    panels, staged, gram_sum, turn_parts, load_sem, store_sem, send_sem, recv_sem,
):
    packed = panels.shape[2]
    me = lax.axis_index("pair")
    factor = lax.axis_index("factor")
    right = lax.rem(me + 1, slots)
    left = lax.rem(me + slots - 1, slots)
    is_first = 1 - (me + slots - 1) // slots
    is_last = (me + 1) // slots

    loads = []
    for which, source in enumerate((x_in, v_in)):
        load = pltpu.make_async_copy(source, staged.at[which], load_sem.at[which])
        load.start()
        loads.append(load)

    barrier = pltpu.get_barrier_semaphore()
    for neighbour in (left, right):
        pl.semaphore_signal(
            barrier, inc=1, device_id=(factor, neighbour), device_id_type=MESH
        )
    pl.semaphore_wait(barrier, 2)

    def place(step, side):
        return 2 * step + side

    def rows_of(chunk):
        return pl.ds(pl.multiple_of(chunk * ROWS, ROWS), ROWS)

    def remote(which, step, chunk, side, device):
        return pltpu.make_async_remote_copy(
            src_ref=panels.at[which, place(step, side), rows_of(chunk)],
            dst_ref=panels.at[which, place(step + 1, side), rows_of(chunk)],
            send_sem=send_sem.at[which, place(step, side), chunk],
            recv_sem=recv_sem.at[which, place(step, side), chunk],
            device_id=(factor, device),
            device_id_type=MESH,
        )

    def to_right(which, step, chunk):
        return remote(which, step, chunk, 0, right)

    def to_left(which, step, chunk):
        return remote(which, step, chunk, 1, left)

    def send(which, step, chunk):
        @pl.when(me < slots - 1)
        def _():
            to_right(which, step, chunk).start()

        @pl.when(me > 0)
        def _():
            to_left(which, step, chunk).start()

    def wait_sent(which, step, chunk):
        @pl.when(me < slots - 1)
        def _():
            to_right(which, step, chunk).wait_send()

        @pl.when(me > 0)
        def _():
            to_left(which, step, chunk).wait_send()

    def wait_received(which, step, chunk):
        @pl.when(me > 0)
        def _():
            to_right(which, step, chunk).wait_recv()

        @pl.when(me < slots - 1)
        def _():
            to_left(which, step, chunk).wait_recv()

    def every_chunk(act):
        def body(chunk, _):
            act(chunk)
            return 0

        lax.fori_loop(0, packed // ROWS, body, 0)

    def pack(which):
        low = iota((ROWS, WIDTH), 1) < HALF

        def body(chunk, _):
            at = pl.ds(pl.multiple_of(chunk * ROWS, ROWS), ROWS)
            other = pl.ds(
                pl.multiple_of(packed + chunk * ROWS, ROWS), ROWS
            )
            one, two = staged[which, at], staged[which, other]
            panels[which, 0, at] = jnp.where(low, one, swap_halves(two))
            panels[which, 1, at] = jnp.where(low, swap_halves(one), two)
            return 0

        lax.fori_loop(0, packed // ROWS, body, 0)

    def unpack(which):
        low = iota((ROWS, WIDTH), 1) < HALF

        def body(chunk, _):
            at = pl.ds(pl.multiple_of(chunk * ROWS, ROWS), ROWS)
            other = pl.ds(
                pl.multiple_of(packed + chunk * ROWS, ROWS), ROWS
            )
            upper = panels[which, place(STEPS, 0), at]
            lower = panels[which, place(STEPS, 1), at]
            staged[which, at] = jnp.where(low, upper, swap_halves(lower))
            staged[which, other] = jnp.where(low, swap_halves(upper), lower)
            return 0

        lax.fori_loop(0, packed // ROWS, body, 0)

    def panel_rows(which, step, at):
        return jnp.concatenate(
            [panels[which, place(step, 0), at], panels[which, place(step, 1), at]], axis=1
        )

    def gram(step):
        gram_sum[...] = jnp.zeros_like(gram_sum)
        inner = lambda a, b: lax.dot_general(
            a, b, (((0,), (0,)), ((), ())), preferred_element_type=F32
        )

        def add(chunk):
            @pl.when(step > 0)
            def _():
                wait_received(0, step - 1, chunk)

            high, low = split(panel_rows(0, step, rows_of(chunk)), 2)
            gram_sum[0] += inner(high, high) + inner(low, low)
            gram_sum[1] += inner(high, low)

        every_chunk(add)
        mixed = gram_sum[1]
        return folded(gram_sum[0] + (mixed + mixed.T))

    def apply(which, step, chunk, terms):
        at = rows_of(chunk)
        high, low = split(panel_rows(which, step, at), 2)
        total = jnp.dot(high, turn_parts[0], preferred_element_type=F32)
        small = jnp.dot(low, turn_parts[0], preferred_element_type=F32)
        for term in range(1, terms):
            small += jnp.dot(high, turn_parts[term], preferred_element_type=F32)
        total += small
        panels[which, place(step, 0) + 3 * is_last, at] = total[:, :WIDTH]
        panels[which, place(step, 1) + is_first, at] = total[:, WIDTH:]

    loads[0].wait()
    pack(0)

    def one_step(step, _):
        sums = gram(step)

        turn = rotations(sums)
        for term, part in enumerate(split(expanded(turn, is_first == 1), 3)):
            turn_parts[term] = part

        def turn_columns(chunk):
            apply(0, step, chunk, 3)
            send(0, step, chunk)

        every_chunk(turn_columns)

        @pl.when(step == 0)
        def _():
            loads[1].wait()
            pack(1)

        def turn_basis(chunk):
            @pl.when(step > 0)
            def _():
                wait_received(1, step - 1, chunk)

            apply(1, step, chunk, 2)
            send(1, step, chunk)

        every_chunk(turn_basis)
        return 0

    lax.fori_loop(0, STEPS, one_step, 0)
    every_chunk(lambda chunk: wait_received(0, STEPS - 1, chunk))

    stores = []
    for which, target in enumerate((x_out, v_out)):
        if which:
            every_chunk(lambda chunk: wait_received(1, STEPS - 1, chunk))
        unpack(which)
        store = pltpu.make_async_copy(staged.at[which], target, store_sem.at[which])
        store.start()
        stores.append(store)

    def settle(step, _):
        for which in range(2):
            every_chunk(lambda chunk: wait_sent(which, step, chunk))
        return 0

    lax.fori_loop(0, STEPS, settle, 0)
    for store in stores:
        store.wait()


def on_device(columns, basis):
    rows, width = columns.shape
    slots = lax.axis_size("pair")
    packed = rows // 2
    shape = jax.ShapeDtypeStruct((rows, width), F32)
    return pl.pallas_call(
        functools.partial(kernel, slots),
        out_shape=(shape, shape),
        in_specs=[pl.BlockSpec(memory_space=pl.ANY)] * 2,
        out_specs=(pl.BlockSpec(memory_space=pl.ANY),) * 2,
        scratch_shapes=[
            pltpu.VMEM((2, 2 * STEPS + 2, packed, width), F32),
            pltpu.VMEM((2, rows, width), F32),
            pltpu.VMEM((2, 2 * width, 2 * width), F32),
            pltpu.VMEM((3, 2 * width, 2 * width), BF16),
            pltpu.SemaphoreType.DMA((2,)),
            pltpu.SemaphoreType.DMA((2,)),
            pltpu.SemaphoreType.DMA((2, 2 * STEPS, packed // ROWS)),
            pltpu.SemaphoreType.DMA((2, 2 * STEPS, packed // ROWS)),
        ],
        compiler_params=pltpu.CompilerParams(
            collective_id=0, has_side_effects=True, vmem_limit_bytes=50 * 2**20
        ),
        cost_estimate=pl.CostEstimate(
            flops=6 * 9 * 2 * rows * width * width,
            bytes_accessed=4 * rows * width * 4,
            transcendentals=0,
        ),
    )(columns, basis)


def solution(mesh):
    spec = P("factor", "pair")
    return jax.shard_map(
        on_device, mesh=mesh, in_specs=(spec, spec), out_specs=(spec, spec), check_vma=False
    )
```

```python
import functools

import jax
import jax.numpy as jnp
from jax import lax
from jax.experimental import pallas as pl
from jax.experimental.pallas import tpu as pltpu
from jax.sharding import PartitionSpec as P

STEPS = 6
INNER_ROUNDS = 8
MESH = pl.DeviceIdType.MESH
F32 = jnp.float32
BF16 = jnp.bfloat16
WIDTH = 128
HALF = 64
ROWS = 512
RING = 8


def iota(shape, dim):
    return lax.broadcasted_iota(jnp.int32, shape, dim)


def rsqrt(value):
    guess = lax.rsqrt(value)
    return guess * (1.5 - 0.5 * value * guess * guess)


def sublane_roll(value, shift):
    return pltpu.roll(value, shift % 8, 0)


def order_of(row, shift):
    inside = lax.rem(row, HALF)
    k = 8 * lax.rem(inside, 8) + inside // 8
    k = jnp.where(row < HALF, k, WIDTH - 1 - k)
    return jnp.where(k == 0, 0, 1 + lax.rem(k - 1 + shift, WIDTH - 1))


def order_matrix(shift):
    rows = iota((WIDTH, WIDTH), 0)
    lanes = iota((WIDTH, WIDTH), 1)
    return jnp.where(order_of(rows, shift) == lanes, 1.0, 0.0).astype(F32)


def moved_on(first, second):
    top = iota((8, first.shape[1]), 0) == 0
    end = iota((8, first.shape[1]), 0) == 7
    a, b = first, second
    new_first = jnp.concatenate(
        [
            jnp.where(top, a[:8], a[8:16]),
            a[16:],
            jnp.where(end, b[HALF - 8:], sublane_roll(a[:8], -1)),
        ],
        axis=0,
    )
    new_second = jnp.concatenate(
        [jnp.where(top, a[8:16], sublane_roll(b[HALF - 8:], 1)), b[:HALF - 8]], axis=0
    )
    return new_first, new_second


def angles(diag_a, diag_b, cross):
    spread = diag_a - diag_b
    twice = 2.0 * cross
    twice = jnp.where(spread >= 0.0, twice, -twice)
    size = jnp.abs(spread)
    most = jnp.maximum(size, jnp.abs(twice))
    still = most == 0.0
    scale = pl.reciprocal(jnp.where(still, 1.0, most), approx=True)
    size = jnp.where(still, 1.0, size * scale)
    twice = twice * scale
    inverse = rsqrt(size * size + twice * twice)
    cos_sq = 0.5 + 0.5 * size * inverse
    inverse_cos = rsqrt(cos_sq)
    return cos_sq * inverse_cos, 0.5 * twice * inverse * inverse_cos


def lane_sum(value):
    return jnp.broadcast_to(jnp.sum(value, axis=1, keepdims=True), value.shape)


def rotations(gram):
    start = order_matrix(0)
    start_bf16 = start.astype(BF16)
    pieces = [jnp.dot(start_bf16, part, preferred_element_type=F32) for part in split(gram, 3)]
    ordered = (pieces[0] + pieces[1]) + pieces[2]
    turn_a, turn_b = start[:HALF], start[HALF:]
    with_a, with_b = ordered[:HALF], ordered[HALF:]
    diag_a, diag_b = lane_sum(turn_a * with_a), lane_sum(turn_b * with_b)
    lanes = iota((HALF, WIDTH), 1)
    waves = jnp.zeros((HALF, WIDTH), F32)
    for round_no in range(INNER_ROUNDS):
        cross = lane_sum(turn_a * with_b)
        cosine, sine = angles(diag_a, diag_b, cross)
        waves = jnp.where(lanes == round_no, cosine, waves)
        waves = jnp.where(lanes == INNER_ROUNDS + round_no, sine, waves)
        turn_a, turn_b = cosine * turn_a + sine * turn_b, cosine * turn_b - sine * turn_a
        if round_no + 1 < INNER_ROUNDS:
            with_a, with_b = cosine * with_a + sine * with_b, cosine * with_b - sine * with_a
            both = 2.0 * cosine * sine * cross
            cos_sq, sin_sq = cosine * cosine, sine * sine
            diag_a, diag_b = (
                cos_sq * diag_a + sin_sq * diag_b + both,
                cos_sq * diag_b + sin_sq * diag_a - both,
            )
            turn_a, turn_b = moved_on(turn_a, turn_b)
            with_a, with_b = moved_on(with_a, with_b)
            diag_a, diag_b = moved_on(diag_a, diag_b)
    pieces = in_order(turn_a, turn_b, 3)
    return (pieces[0] + pieces[1]) + pieces[2], waves


def in_order(turn_a, turn_b, parts):
    end = order_matrix(INNER_ROUNDS - 1).astype(BF16)
    turn = jnp.concatenate([turn_a, turn_b], axis=0)
    return [
        lax.dot_general(part, end, (((0,), (0,)), ((), ())), preferred_element_type=F32)
        for part in split(turn, parts)
    ]


def multiplied_out(waves):
    columns = jnp.concatenate([waves] * (WIDTH // 16), axis=0).T
    start = order_matrix(0)
    turn_a, turn_b = start[:HALF], start[HALF:]
    for round_no in range(INNER_ROUNDS):
        wide = lambda at: jnp.broadcast_to(columns[:HALF, at:at + 1], (HALF, WIDTH))
        cosine, sine = wide(round_no), wide(INNER_ROUNDS + round_no)
        turn_a, turn_b = cosine * turn_a + sine * turn_b, cosine * turn_b - sine * turn_a
        if round_no + 1 < INNER_ROUNDS:
            turn_a, turn_b = moved_on(turn_a, turn_b)
    return in_order(turn_a, turn_b, 2)


def swap_halves(value):
    return pltpu.roll(value, HALF, 1)


def split(value, parts):
    out = []
    for _ in range(parts - 1):
        part = value.astype(BF16)
        out.append(part)
        value = value - part.astype(F32)
    out.append(value.astype(BF16))
    return out


def folded(big):
    low = iota((HALF, WIDTH), 1) < HALF
    halves = []
    for at in (0, WIDTH):
        one, two = big[at:at + HALF], big[at + HALF:at + WIDTH]
        left = one[:, :WIDTH] + swap_halves(two[:, :WIDTH])
        right = swap_halves(one[:, WIDTH:]) + two[:, WIDTH:]
        halves.append(jnp.where(low, left, right))
    return jnp.concatenate(halves, axis=0)


def expanded(turn, is_first):
    low = iota((HALF, WIDTH), 1) < HALF
    out = []
    for at in (0, HALF):
        rows = turn[at:at + HALF]
        moved = swap_halves(rows)
        for keep in (low, ~low):
            to_upper = jnp.where(keep, rows if keep is low else moved, 0.0)
            to_lower = jnp.where(keep, moved if keep is low else rows, 0.0)
            one = jnp.where(is_first, to_lower, to_upper)
            two = jnp.where(is_first, to_upper, to_lower)
            out.append(jnp.concatenate([one, two], axis=1))
    return jnp.concatenate(out, axis=0)


def loop(low, high, act):
    def body(at, _):
        act(at)
        return 0

    lax.fori_loop(low, high, body, 0)


def kernel(
    slots, x_in, v_in, x_out, v_out,
    panels, staged, gram_sum, turn_parts, held, moving, edge_out, edge_in, waves, weights,
    load_sem, store_sem, send_sem, recv_sem, out_send, in_recv,
    edge_send, edge_recv, wave_send, wave_recv, passing, hop_send, hop_recv, pass_send,
):
    packed = panels.shape[1]
    share = held.shape[1]
    bend = share // 2
    chunks = packed // ROWS
    me = lax.axis_index("pair")
    factor = lax.axis_index("factor")
    right = lax.rem(me + 1, slots)
    left = lax.rem(me + slots - 1, slots)
    is_first = 1 - (me + slots - 1) // slots
    is_last = (me + 1) // slots
    own = lax.rem(me, RING)
    base = me - own
    twin = own + 1 - 2 * lax.rem(own, 2)
    ring_right = lax.rem(me + RING, slots)
    ring_left = lax.rem(me + slots - RING, slots)
    first_ring = me < RING
    last_ring = me >= slots - RING

    def other(offset):
        return lax.rem(own + offset, RING)

    def remote(src, dst, send, recv, device):
        return pltpu.make_async_remote_copy(
            src_ref=src, dst_ref=dst, send_sem=send, recv_sem=recv,
            device_id=(factor, device), device_id_type=MESH,
        )

    def rows_of(chunk, size=ROWS):
        return pl.ds(pl.multiple_of(chunk * size, size), size)

    def place(step, side):
        return 2 * step + side

    def block(step, chunk, side, device):
        at = place(step, side)
        return remote(
            panels.at[at, rows_of(chunk)], panels.at[at + 2, rows_of(chunk)],
            send_sem.at[at, chunk], recv_sem.at[at, chunk], device,
        )

    def send_block(step, chunk):
        @pl.when(me < slots - 1)
        def _():
            block(step, chunk, 0, right).start()

        @pl.when(me > 0)
        def _():
            block(step, chunk, 1, left).start()

    def wait_sent(step, chunk):
        @pl.when(me < slots - 1)
        def _():
            block(step, chunk, 0, right).wait_send()

        @pl.when(me > 0)
        def _():
            block(step, chunk, 1, left).wait_send()

    def wait_received(step, chunk):
        @pl.when(me > 0)
        def _():
            block(step, chunk, 0, right).wait_recv()

        @pl.when(me < slots - 1)
        def _():
            block(step, chunk, 1, left).wait_recv()

    above, below = other(2), other(6)
    above_twin, below_twin = lax.rem(twin + 2, RING), lax.rem(twin + 6, RING)
    opposite = (other(4), lax.rem(twin + 4, RING))
    hop_to = (above, below)
    hop_from = (below, above)
    pass_to = (above, below_twin)

    def rows_from(way, peer):
        return held.at[peer] if way else v_in.at[rows_of(peer, share)]

    def rows_at(way, row):
        return v_out.at[rows_of(row, share)] if way else held.at[row]

    def piece(way, peer, lands):
        return remote(
            rows_from(way, peer), rows_at(way, lands),
            out_send.at[way, peer], in_recv.at[way, lands], base + peer,
        )

    def hop(way, side):
        return remote(
            rows_from(way, opposite[side]), passing.at[way, side],
            hop_send.at[way, side], hop_recv.at[way, side], base + hop_to[side],
        )

    def pass_on(way, side):
        return remote(
            passing.at[way, side], rows_at(way, hop_from[side]),
            pass_send.at[way, side], in_recv.at[way, hop_from[side]], base + pass_to[side],
        )

    def send_piece(way, peer):
        piece(way, peer, own).start()

    def forward(way):
        for side in range(2):
            hop(way, side).wait_recv()
            pass_on(way, side).start()

    def wait_pieces(way):
        loop(1, RING, lambda o: piece(way, other(o), other(o)).wait_recv())

    def wait_pieces_sent(way):
        for peer in (above, below, above_twin, below_twin, twin):
            piece(way, peer, own).wait_send()
        for side in range(2):
            hop(way, side).wait_send()
            pass_on(way, side).wait_send()

    def wave(step, peer, lands):
        return remote(
            waves.at[step, lands], waves.at[step, lands],
            wave_send.at[step, peer], wave_recv.at[step, lands], base + peer,
        )

    def edge(step, side, device):
        return remote(
            edge_out.at[step, side], edge_in.at[step, side],
            edge_send.at[step, side], edge_recv.at[step, side], device,
        )

    def to_edges(act_right, act_left):
        pl.when(jnp.logical_not(last_ring))(act_right)
        pl.when(jnp.logical_not(first_ring))(act_left)

    load = pltpu.make_async_copy(x_in, staged, load_sem.at[0])
    load.start()
    keep_in = pltpu.make_async_copy(
        v_in.at[rows_of(own, share)], held.at[own], load_sem.at[1]
    )
    keep_in.start()

    barrier = pltpu.get_barrier_semaphore()
    for offset in range(1, RING):
        pl.semaphore_signal(
            barrier, inc=1, device_id=(factor, base + other(offset)), device_id_type=MESH
        )
    for neighbour in (left, right, ring_left, ring_right):
        pl.semaphore_signal(
            barrier, inc=1, device_id=(factor, neighbour), device_id_type=MESH
        )
    pl.semaphore_wait(barrier, RING + 3)

    for side in range(2):
        hop(0, side).start()
    send_piece(0, twin)

    def pack():
        low = iota((ROWS, WIDTH), 1) < HALF

        def one(chunk):
            upper, lower = staged[rows_of(chunk)], staged[rows_of(chunk + chunks)]
            panels[0, rows_of(chunk)] = jnp.where(low, upper, swap_halves(lower))
            panels[1, rows_of(chunk)] = jnp.where(low, swap_halves(upper), lower)

        loop(0, chunks, one)

    def unpack():
        low = iota((ROWS, WIDTH), 1) < HALF

        def one(chunk):
            upper = panels[place(STEPS, 0), rows_of(chunk)]
            lower = panels[place(STEPS, 1), rows_of(chunk)]
            staged[rows_of(chunk)] = jnp.where(low, upper, swap_halves(lower))
            staged[rows_of(chunk + chunks)] = jnp.where(low, swap_halves(upper), lower)

        loop(0, chunks, one)

    def panel_rows(step, at):
        return jnp.concatenate(
            [panels[place(step, 0), at], panels[place(step, 1), at]], axis=1
        )

    def gram(step):
        gram_sum[...] = jnp.zeros_like(gram_sum)
        inner = lambda a, b: lax.dot_general(
            a, b, (((0,), (0,)), ((), ())), preferred_element_type=F32
        )

        def add(chunk):
            @pl.when(step > 0)
            def _():
                wait_received(step - 1, chunk)

            @pl.when(chunk == chunks - 1)
            def _():
                @pl.when(step == 1)
                def _():
                    send_piece(0, above)
                    send_piece(0, below)

                @pl.when(step == 2)
                def _():
                    forward(0)

                @pl.when(step == 3)
                def _():
                    send_piece(0, above_twin)
                    send_piece(0, below_twin)

            high, low = split(panel_rows(step, rows_of(chunk)), 2)
            gram_sum[0] += inner(high, high) + inner(low, low)
            gram_sum[1] += inner(high, low)

        loop(0, chunks, add)
        mixed = gram_sum[1]
        return folded(gram_sum[0] + (mixed + mixed.T))

    def apply(step, chunk):
        at = rows_of(chunk)
        high, low = split(panel_rows(step, at), 2)
        dot = lambda a, term: jnp.dot(a, turn_parts[term], preferred_element_type=F32)
        total = dot(high, 0) + (dot(low, 0) + dot(high, 1) + dot(high, 2))
        panels[place(step, 0) + 3 * is_last, at] = total[:, :WIDTH]
        panels[place(step, 1) + is_first, at] = total[:, WIDTH:]

    low_lanes = iota((share, WIDTH), 1) < HALF
    low_bend = iota((bend, WIDTH), 1) < HALF

    def spread_held():
        def one(k):
            upper = held[jnp.minimum(k, RING - 1)]
            lower = held[jnp.maximum(k - 2, 0)]
            moving[0, k] = jnp.where(low_lanes, upper, lower)

        loop(0, RING + 2, one)

    def slot_rows(now, slot):
        return jnp.where(low_lanes, moving[now, slot], moving[now, slot + 2])

    def prepare(step):
        def one(slot):
            @pl.when(slot != own)
            def _():
                wave(step, slot, slot).wait_recv()

            high, low = multiplied_out(waves[step, slot])
            first_slot = first_ring & (slot == 0)
            high = jnp.where(first_slot, swap_halves(high), high)
            low = jnp.where(first_slot, swap_halves(low), low)
            weights[step, slot] = jnp.concatenate([high, low], axis=1).astype(BF16)

        loop(0, RING, one)

    def take_edges(step, now):
        def from_left():
            edge(step, 0, ring_right).wait_recv()
            got = edge_in[step, 0]
            moving[now, 0, :bend] = got
            moving[now, 0, bend:] = swap_halves(got)

        def from_right():
            edge(step, 1, ring_left).wait_recv()
            got = edge_in[step, 1]
            moving[now, RING + 1, :bend] = swap_halves(got)
            moving[now, RING + 1, bend:] = got

        pl.when(jnp.logical_not(first_ring))(from_left)
        pl.when(jnp.logical_not(last_ring))(from_right)

    def turn_basis(step):
        now = lax.rem(step, 2)
        later = 1 - now

        def one(slot):
            high, low = split(slot_rows(now, slot), 2)
            weight = weights[step, slot]
            both = jnp.dot(
                jnp.concatenate([high, low], axis=1),
                jnp.concatenate([weight, weight], axis=0),
                preferred_element_type=F32,
            )
            moving[later, slot + 1] = both[:, :WIDTH] + both[:, WIDTH:]

        loop(1, RING - 1, one)
        pl.when(step > 0)(lambda: take_edges(step - 1, now))
        loop(0, 2, lambda side: one(side * (RING - 1)))

        def up():
            give = moving[later, RING]
            edge_out[step, 0] = jnp.where(low_bend, give[:bend], swap_halves(give[bend:]))
            edge(step, 0, ring_right).start()

        def down():
            give = moving[later, 1]
            edge_out[step, 1] = jnp.where(low_bend, swap_halves(give[:bend]), give[bend:])
            edge(step, 1, ring_left).start()

        to_edges(up, down)

        @pl.when(first_ring)
        def _():
            moving[later, 0] = swap_halves(moving[later, 1])

        @pl.when(last_ring)
        def _():
            moving[later, RING + 1] = swap_halves(moving[later, RING])

    load.wait()
    pack()

    def one_step(step):
        turn, own_waves = rotations(gram(step))
        for term, part in enumerate(split(expanded(turn, is_first == 1), 3)):
            turn_parts[term] = part

        def turn_columns(chunk):
            apply(step, chunk)
            send_block(step, chunk)

        loop(0, chunks, turn_columns)
        blank = jnp.zeros((HALF, WIDTH), F32)
        waves[step, own] = jnp.concatenate([own_waves, blank], axis=0).T[:16]
        loop(1, RING, lambda offset: wave(step, other(offset), own).start())

        loop(step - (step + 5) // 6, step + step // 5, prepare)

        @pl.when(step == 3)
        def _():
            keep_in.wait()
            wait_pieces(0)
            spread_held()

        loop((step // 4) * 2 + (step // 5) * 2, (step // 3 + step // 4 + step // 5) * 2, turn_basis)

    loop(0, STEPS, one_step)

    def gather_rows(slot):
        held[slot] = slot_rows(STEPS % 2, slot)

    take_edges(STEPS - 1, STEPS % 2)
    for side in range(2):
        gather_rows(opposite[side])
        hop(1, side).start()
    for peer in (above, below, above_twin, below_twin, twin):
        gather_rows(peer)
        send_piece(1, peer)
    gather_rows(own)
    keep_out = pltpu.make_async_copy(
        held.at[own], v_out.at[rows_of(own, share)], store_sem.at[1]
    )
    keep_out.start()

    loop(0, chunks, lambda chunk: wait_received(STEPS - 1, chunk))
    unpack()
    store = pltpu.make_async_copy(staged, x_out, store_sem.at[0])
    store.start()

    forward(1)

    def settle(step):
        loop(0, chunks, lambda chunk: wait_sent(step, chunk))
        loop(1, RING, lambda o: wave(step, other(o), own).wait_send())
        to_edges(
            lambda: edge(step, 0, ring_right).wait_send(),
            lambda: edge(step, 1, ring_left).wait_send(),
        )

    loop(0, STEPS, settle)
    wait_pieces_sent(0)
    wait_pieces_sent(1)
    wait_pieces(1)
    store.wait()
    keep_out.wait()


def on_device(columns, basis):
    rows, width = columns.shape
    slots = lax.axis_size("pair")
    packed = rows // 2
    share = rows // RING
    shape = jax.ShapeDtypeStruct((rows, width), F32)
    dma = pltpu.SemaphoreType.DMA
    return pl.pallas_call(
        functools.partial(kernel, slots),
        out_shape=(shape, shape),
        in_specs=[pl.BlockSpec(memory_space=pl.ANY)] * 2,
        out_specs=(pl.BlockSpec(memory_space=pl.ANY),) * 2,
        scratch_shapes=[
            pltpu.VMEM((2 * STEPS + 2, packed, width), F32),
            pltpu.VMEM((rows, width), F32),
            pltpu.VMEM((2, 2 * width, 2 * width), F32),
            pltpu.VMEM((3, 2 * width, 2 * width), BF16),
            pltpu.VMEM((RING, share, width), F32),
            pltpu.VMEM((2, RING + 2, share, width), F32),
            pltpu.VMEM((STEPS, 2, share // 2, width), F32),
            pltpu.VMEM((STEPS, 2, share // 2, width), F32),
            pltpu.VMEM((STEPS, RING, 16, width), F32),
            pltpu.VMEM((STEPS, RING, width, 2 * width), BF16),
            dma((2,)),
            dma((2,)),
            dma((2 * STEPS, packed // ROWS)),
            dma((2 * STEPS, packed // ROWS)),
            dma((2, RING)),
            dma((2, RING)),
            dma((STEPS, 2)),
            dma((STEPS, 2)),
            dma((STEPS, RING)),
            dma((STEPS, RING)),
            pltpu.VMEM((2, 2, share, width), F32),
            dma((2, 2)),
            dma((2, 2)),
            dma((2, 2)),
        ],
        compiler_params=pltpu.CompilerParams(
            collective_id=0, has_side_effects=True, vmem_limit_bytes=50 * 2**20
        ),
        cost_estimate=pl.CostEstimate(
            flops=6 * 9 * 2 * rows * width * width,
            bytes_accessed=4 * rows * width * 4,
            transcendentals=0,
        ),
    )(columns, basis)


def solution(mesh):
    spec = P("factor", "pair")
    return jax.shard_map(
        on_device, mesh=mesh, in_specs=(spec, spec), out_specs=(spec, spec), check_vma=False
    )
```

```python
import functools

import jax
import jax.numpy as jnp
from jax import lax
from jax.experimental import pallas as pl
from jax.experimental.pallas import tpu as pltpu
from jax.sharding import PartitionSpec as P

STEPS = 6
INNER_ROUNDS = 8
MESH = pl.DeviceIdType.MESH
F32 = jnp.float32
BF16 = jnp.bfloat16
WIDTH = 128
HALF = 64
LONG = 1024
RING = 8


def iota(shape, dim):
    return lax.broadcasted_iota(jnp.int32, shape, dim)


def rsqrt(value):
    guess = lax.rsqrt(value)
    return guess * (1.5 - 0.5 * value * guess * guess)


def sublane_roll(value, shift):
    return pltpu.roll(value, shift % 8, 0)


def order_of(row, shift):
    inside = lax.rem(row, HALF)
    k = 8 * lax.rem(inside, 8) + inside // 8
    k = jnp.where(row < HALF, k, WIDTH - 1 - k)
    return jnp.where(k == 0, 0, 1 + lax.rem(k - 1 + shift, WIDTH - 1))


def moved_on(first, second):
    top = iota((8, first.shape[1]), 0) == 0
    end = iota((8, first.shape[1]), 0) == 7
    a, b = first, second
    new_first = jnp.concatenate(
        [
            jnp.where(top, a[:8], a[8:16]),
            a[16:],
            jnp.where(end, b[HALF - 8:], sublane_roll(a[:8], -1)),
        ],
        axis=0,
    )
    new_second = jnp.concatenate(
        [jnp.where(top, a[8:16], sublane_roll(b[HALF - 8:], 1)), b[:HALF - 8]], axis=0
    )
    return new_first, new_second


def angles(diag_a, diag_b, cross):
    spread = diag_a - diag_b
    twice = 2.0 * cross
    twice = jnp.where(spread >= 0.0, twice, -twice)
    size = jnp.abs(spread)
    most = jnp.maximum(size, jnp.abs(twice))
    still = most == 0.0
    scale = pl.reciprocal(jnp.where(still, 1.0, most), approx=True)
    size = jnp.where(still, 1.0, size * scale)
    twice = twice * scale
    inverse = rsqrt(size * size + twice * twice)
    cos_sq = 0.5 + 0.5 * size * inverse
    inverse_cos = rsqrt(cos_sq)
    return cos_sq * inverse_cos, 0.5 * twice * inverse * inverse_cos


def lane_sum(value):
    return jnp.broadcast_to(jnp.sum(value, axis=1, keepdims=True), value.shape)


def rotations(gram, start):
    order = start.astype(BF16)
    pieces = [jnp.dot(order, part, preferred_element_type=F32) for part in split(gram, 3)]
    ordered = (pieces[0] + pieces[1]) + pieces[2]
    turn_a, turn_b = start[:HALF], start[HALF:]
    with_a, with_b = ordered[:HALF], ordered[HALF:]
    diag_a, diag_b = lane_sum(turn_a * with_a), lane_sum(turn_b * with_b)
    lanes = iota((HALF, WIDTH), 1)
    waves = jnp.zeros((HALF, WIDTH), F32)
    for round_no in range(INNER_ROUNDS):
        cross = lane_sum(turn_a * with_b)
        cosine, sine = angles(diag_a, diag_b, cross)
        waves = jnp.where(lanes == round_no, cosine, waves)
        waves = jnp.where(lanes == INNER_ROUNDS + round_no, sine, waves)
        turn_a, turn_b = cosine * turn_a + sine * turn_b, cosine * turn_b - sine * turn_a
        if round_no + 1 < INNER_ROUNDS:
            with_a, with_b = cosine * with_a + sine * with_b, cosine * with_b - sine * with_a
            both = 2.0 * cosine * sine * cross
            cos_sq, sin_sq = cosine * cosine, sine * sine
            diag_a, diag_b = (
                cos_sq * diag_a + sin_sq * diag_b + both,
                cos_sq * diag_b + sin_sq * diag_a - both,
            )
            turn_a, turn_b = moved_on(turn_a, turn_b)
            with_a, with_b = moved_on(with_a, with_b)
            diag_a, diag_b = moved_on(diag_a, diag_b)
    return jnp.concatenate([turn_a, turn_b], axis=0), waves


def final_order(swapped):
    rows = iota((WIDTH, WIDTH), 0)
    rows = lax.rem(rows + HALF, WIDTH) if swapped else rows
    lanes = iota((WIDTH, WIDTH), 1)
    return jnp.where(order_of(lanes, INNER_ROUNDS - 1) == rows, 1.0, 0.0).astype(BF16)


def in_order(turn, order, parts):
    return [
        jnp.dot(order, part, preferred_element_type=F32).astype(BF16)
        for part in split(turn, parts)
    ]


def swap_halves(value):
    return pltpu.roll(value, HALF, 1)


def split(value, parts):
    out = []
    for _ in range(parts - 1):
        part = value.astype(BF16)
        out.append(part)
        value = value - part.astype(F32)
    out.append(value.astype(BF16))
    return out


def loop(low, high, act):
    def body(at, _):
        act(at)
        return 0

    lax.fori_loop(low, high, body, 0)


def kernel(
    slots, x_in, v_in, x_out, v_out,
    panels, staged, parts_of, gram_sum, turn_parts, start, order, spread, wide,
    held, moving, edge_out, edge_in, waves, weights,
    load_sem, store_sem, keep_sem, send_sem, recv_sem, out_send, in_recv,
    edge_send, edge_recv, wave_send, wave_recv, passing, hop_send, hop_recv, pass_send,
):
    share = held.shape[1]
    bend = share // 2
    chunks, _, length = panels.shape[1:]
    me = lax.axis_index("pair")
    factor = lax.axis_index("factor")
    right = lax.rem(me + 1, slots)
    left = lax.rem(me + slots - 1, slots)
    is_first = 1 - (me + slots - 1) // slots
    is_last = (me + 1) // slots
    own = lax.rem(me, RING)
    base = me - own
    twin = own + 1 - 2 * lax.rem(own, 2)
    ring_right = lax.rem(me + RING, slots)
    ring_left = lax.rem(me + slots - RING, slots)
    first_ring = me < RING
    last_ring = me >= slots - RING

    def other(offset):
        return lax.rem(own + offset, RING)

    def remote(src, dst, send, recv, device):
        return pltpu.make_async_remote_copy(
            src_ref=src, dst_ref=dst, send_sem=send, recv_sem=recv,
            device_id=(factor, device), device_id_type=MESH,
        )

    def rows_of(chunk, size):
        return pl.ds(pl.multiple_of(chunk * size, size), size)

    def place(step, side):
        return 2 * step + side

    def block(step, chunk, side, device):
        at = place(step, side)
        return remote(
            panels.at[at, chunk], panels.at[at + 2, chunk],
            send_sem.at[at, chunk], recv_sem.at[at, chunk], device,
        )

    def send_block(step, chunk):
        @pl.when(me < slots - 1)
        def _():
            block(step, chunk, 0, right).start()

        @pl.when(me > 0)
        def _():
            block(step, chunk, 1, left).start()

    def wait_sent(step, chunk):
        @pl.when(me < slots - 1)
        def _():
            block(step, chunk, 0, right).wait_send()

        @pl.when(me > 0)
        def _():
            block(step, chunk, 1, left).wait_send()

    def wait_received(step, chunk):
        @pl.when(me > 0)
        def _():
            block(step, chunk, 0, right).wait_recv()

        @pl.when(me < slots - 1)
        def _():
            block(step, chunk, 1, left).wait_recv()

    above, below = other(2), other(6)
    above_twin, below_twin = lax.rem(twin + 2, RING), lax.rem(twin + 6, RING)
    opposite = (other(4), lax.rem(twin + 4, RING))
    hop_to = (above, below)
    hop_from = (below, above)
    pass_to = (above, below_twin)

    def rows_from(way, peer):
        return held.at[peer] if way else v_in.at[rows_of(peer, share)]

    def rows_at(way, row):
        return v_out.at[rows_of(row, share)] if way else held.at[row]

    def piece(way, peer, lands):
        return remote(
            rows_from(way, peer), rows_at(way, lands),
            out_send.at[way, peer], in_recv.at[way, lands], base + peer,
        )

    def hop(way, side):
        return remote(
            rows_from(way, opposite[side]), passing.at[way, side],
            hop_send.at[way, side], hop_recv.at[way, side], base + hop_to[side],
        )

    def pass_on(way, side):
        return remote(
            passing.at[way, side], rows_at(way, hop_from[side]),
            pass_send.at[way, side], in_recv.at[way, hop_from[side]], base + pass_to[side],
        )

    def send_piece(way, peer):
        piece(way, peer, own).start()

    def forward(way):
        for side in range(2):
            hop(way, side).wait_recv()
            pass_on(way, side).start()

    def wait_pieces(way):
        loop(1, RING, lambda o: piece(way, other(o), other(o)).wait_recv())

    def wait_pieces_sent(way):
        for peer in (above, below, above_twin, below_twin, twin):
            piece(way, peer, own).wait_send()
        for side in range(2):
            hop(way, side).wait_send()
            pass_on(way, side).wait_send()

    def wave(step, peer, lands):
        return remote(
            waves.at[step, lands], waves.at[step, lands],
            wave_send.at[step, peer], wave_recv.at[step, lands], base + peer,
        )

    def edge(step, side, device):
        return remote(
            edge_out.at[step, side], edge_in.at[step, side],
            edge_send.at[step, side], edge_recv.at[step, side], device,
        )

    def to_edges(act_right, act_left):
        pl.when(jnp.logical_not(last_ring))(act_right)
        pl.when(jnp.logical_not(first_ring))(act_left)

    def load(chunk):
        at = rows_of(chunk, length)
        return pltpu.make_async_copy(x_in.at[at], staged.at[at], load_sem.at[chunk])

    def store(chunk):
        at = rows_of(chunk, length)
        return pltpu.make_async_copy(staged.at[at], x_out.at[at], store_sem.at[chunk])

    keep_in = pltpu.make_async_copy(
        v_in.at[rows_of(own, share)], held.at[own], keep_sem.at[0]
    )
    keep_out = pltpu.make_async_copy(
        held.at[own], v_out.at[rows_of(own, share)], keep_sem.at[1]
    )
    loop(0, chunks, lambda chunk: load(chunk).start())
    keep_in.start()

    barrier = pltpu.get_barrier_semaphore()
    for offset in range(1, RING):
        pl.semaphore_signal(
            barrier, inc=1, device_id=(factor, base + other(offset)), device_id_type=MESH
        )
    for neighbour in (left, right, ring_left, ring_right):
        pl.semaphore_signal(
            barrier, inc=1, device_id=(factor, neighbour), device_id_type=MESH
        )
    pl.semaphore_wait(barrier, RING + 3)

    for side in range(2):
        hop(0, side).start()
    send_piece(0, twin)

    rows = iota((WIDTH, WIDTH), 0)
    lanes = iota((WIDTH, WIDTH), 1)
    start[...] = jnp.where(order_of(rows, 0) == lanes, 1.0, 0.0).astype(F32)
    for swapped in range(2):
        order[swapped] = final_order(swapped)
    for line in range(16):
        picked = lax.rem(iota((2 * WIDTH, WIDTH), 0), 16) == line
        spread[:, line * WIDTH:(line + 1) * WIDTH] = jnp.where(picked, 1.0, 0.0).astype(BF16)

    def gram(step):
        gram_sum[...] = jnp.zeros_like(gram_sum)

        def add(chunk, panel):
            both = jnp.concatenate(split(panel, 2), axis=0)
            parts_of[chunk] = both
            gram_sum[...] += lax.dot_general(
                both, both, (((1,), (1,)), ((), ())), preferred_element_type=F32
            )

        def first(chunk):
            load(chunk).wait()
            add(chunk, staged[rows_of(chunk, length)].T)

        def later(chunk):
            wait_received(step - 1, chunk)

            @pl.when(chunk == chunks - 1)
            def _():
                @pl.when(step == 1)
                def _():
                    send_piece(0, above)
                    send_piece(0, below)

                @pl.when(step == 2)
                def _():
                    forward(0)

                @pl.when(step == 3)
                def _():
                    send_piece(0, above_twin)
                    send_piece(0, below_twin)

            upper, lower = panels[place(step, 0), chunk], panels[place(step, 1), chunk]
            add(chunk, jnp.concatenate([upper, lower], axis=0))

        pl.when(step == 0)(lambda: loop(0, chunks, first))
        pl.when(step > 0)(lambda: loop(0, chunks, later))
        total = gram_sum[...]
        left_sum = total[:WIDTH, :WIDTH] + (total[:WIDTH, WIDTH:] + total[WIDTH:, WIDTH:])
        return left_sum + total[WIDTH:, :WIDTH]

    def apply(step, chunk):
        out = jnp.dot(turn_parts[...], parts_of[chunk], preferred_element_type=F32)
        out = out[:WIDTH] + (out[WIDTH:2 * WIDTH] + out[2 * WIDTH:])
        panels[place(step, 0) + 3 * is_last, chunk] = out[:HALF]
        panels[place(step, 1) + is_first, chunk] = out[HALF:]

    def unpack(chunk):
        wait_received(STEPS - 1, chunk)
        upper, lower = panels[place(STEPS, 0), chunk], panels[place(STEPS, 1), chunk]
        staged[rows_of(chunk, length)] = jnp.concatenate([upper, lower], axis=0).T
        store(chunk).start()

    low_lanes = iota((share, WIDTH), 1) < HALF
    low_bend = iota((bend, WIDTH), 1) < HALF

    def spread_held():
        def one(k):
            upper = held[jnp.minimum(k, RING - 1)]
            lower = held[jnp.maximum(k - 2, 0)]
            moving[0, k] = jnp.where(low_lanes, upper, lower)

        loop(0, RING + 2, one)

    def slot_rows(now, slot):
        return jnp.where(low_lanes, moving[now, slot], moving[now, slot + 2])

    def prepare(step):
        def arrive(offset):
            slot = other(offset)
            wave(step, slot, slot).wait_recv()

        loop(1, RING, arrive)
        columns = waves[step].reshape(WIDTH, WIDTH).T[:HALF]
        high, low = split(columns, 2)
        both = jnp.concatenate([high, low], axis=1)
        slot_of = lax.rem(iota((HALF, 2 * WIDTH), 1), WIDTH) // 16
        apart = [jnp.where(slot_of == slot, both, 0).astype(BF16) for slot in range(RING)]
        wide[...] = jnp.dot(
            jnp.concatenate(apart, axis=0), spread[...], preferred_element_type=F32
        )

        def one(slot):
            at = rows_of(slot, HALF)
            turn_a, turn_b = start[:HALF], start[HALF:]
            for round_no in range(INNER_ROUNDS):
                line = lambda n: wide[at, n * WIDTH:(n + 1) * WIDTH]
                cosine, sine = line(round_no), line(INNER_ROUNDS + round_no)
                turn_a, turn_b = cosine * turn_a + sine * turn_b, cosine * turn_b - sine * turn_a
                if round_no + 1 < INNER_ROUNDS:
                    turn_a, turn_b = moved_on(turn_a, turn_b)
            swapped = (1 - (me + slots - RING) // slots) * (1 - (slot + RING - 1) // RING)
            turn = jnp.concatenate([turn_a, turn_b], axis=0)
            weights[step, slot] = jnp.concatenate(in_order(turn, order[swapped], 2), axis=0)

        def two(pair):
            one(2 * pair)
            one(2 * pair + 1)

        loop(0, RING // 2, two)

    def take_edges(step, now):
        def from_left():
            edge(step, 0, ring_right).wait_recv()
            got = edge_in[step, 0]
            moving[now, 0, :bend] = got
            moving[now, 0, bend:] = swap_halves(got)

        def from_right():
            edge(step, 1, ring_left).wait_recv()
            got = edge_in[step, 1]
            moving[now, RING + 1, :bend] = swap_halves(got)
            moving[now, RING + 1, bend:] = got

        pl.when(jnp.logical_not(first_ring))(from_left)
        pl.when(jnp.logical_not(last_ring))(from_right)

    def turn_basis(step):
        now = lax.rem(step, 2)
        later = 1 - now

        def one(slot):
            high, low = split(slot_rows(now, slot), 2)
            weight = weights[step, slot]
            both = lax.dot_general(
                jnp.concatenate([high, low], axis=1),
                jnp.concatenate([weight, weight], axis=1),
                (((1,), (1,)), ((), ())),
                preferred_element_type=F32,
            )
            moving[later, slot + 1] = both[:, :WIDTH] + both[:, WIDTH:]

        loop(1, RING - 1, one)
        pl.when(step > 0)(lambda: take_edges(step - 1, now))
        loop(0, 2, lambda side: one(side * (RING - 1)))

        def up():
            give = moving[later, RING]
            edge_out[step, 0] = jnp.where(low_bend, give[:bend], swap_halves(give[bend:]))
            edge(step, 0, ring_right).start()

        def down():
            give = moving[later, 1]
            edge_out[step, 1] = jnp.where(low_bend, swap_halves(give[:bend]), give[bend:])
            edge(step, 1, ring_left).start()

        to_edges(up, down)

        @pl.when(first_ring)
        def _():
            moving[later, 0] = swap_halves(moving[later, 1])

        @pl.when(last_ring)
        def _():
            moving[later, RING + 1] = swap_halves(moving[later, RING])

    def one_step(step):
        turn, own_waves = rotations(gram(step), start[...])
        parts = in_order(turn, order[is_first], 3)
        for at, part in enumerate(parts):
            again = part if at < 2 else jnp.zeros_like(part)
            turn_parts[at * WIDTH:(at + 1) * WIDTH] = jnp.concatenate([part, again], axis=1)

        def turn_columns(chunk):
            apply(step, chunk)
            send_block(step, chunk)

        loop(0, chunks, turn_columns)
        blank = jnp.zeros((HALF, WIDTH), F32)
        waves[step, own] = jnp.concatenate([own_waves, blank], axis=0).T[:16]
        loop(1, RING, lambda offset: wave(step, other(offset), own).start())

        loop(step - (step + 5) // 6, step + step // 5, prepare)

        @pl.when(step == 3)
        def _():
            keep_in.wait()
            wait_pieces(0)
            spread_held()

        loop((step // 4) * 2 + (step // 5) * 2, (step // 3 + step // 4 + step // 5) * 2, turn_basis)

    loop(0, STEPS, one_step)

    def gather_rows(slot):
        held[slot] = slot_rows(STEPS % 2, slot)

    take_edges(STEPS - 1, STEPS % 2)
    for side in range(2):
        gather_rows(opposite[side])
        hop(1, side).start()
    for peer in (above, below, above_twin, below_twin, twin):
        gather_rows(peer)
        send_piece(1, peer)
    gather_rows(own)
    keep_out.start()
    loop(0, chunks, unpack)
    forward(1)

    def settle(step):
        loop(0, chunks, lambda chunk: wait_sent(step, chunk))
        loop(1, RING, lambda o: wave(step, other(o), own).wait_send())
        to_edges(
            lambda: edge(step, 0, ring_right).wait_send(),
            lambda: edge(step, 1, ring_left).wait_send(),
        )

    loop(0, STEPS, settle)
    wait_pieces_sent(0)
    wait_pieces_sent(1)
    wait_pieces(1)
    loop(0, chunks, lambda chunk: store(chunk).wait())
    keep_out.wait()


def on_device(columns, basis):
    rows, width = columns.shape
    slots = lax.axis_size("pair")
    length = min(LONG, rows)
    chunks = rows // length
    share = rows // RING
    shape = jax.ShapeDtypeStruct((rows, width), F32)
    dma = pltpu.SemaphoreType.DMA
    return pl.pallas_call(
        functools.partial(kernel, slots),
        out_shape=(shape, shape),
        in_specs=[pl.BlockSpec(memory_space=pl.ANY)] * 2,
        out_specs=(pl.BlockSpec(memory_space=pl.ANY),) * 2,
        scratch_shapes=[
            pltpu.VMEM((2 * STEPS + 2, chunks, width // 2, length), F32),
            pltpu.VMEM((rows, width), F32),
            pltpu.VMEM((chunks, 2 * width, length), BF16),
            pltpu.VMEM((2 * width, 2 * width), F32),
            pltpu.VMEM((3 * width, 2 * width), BF16),
            pltpu.VMEM((width, width), F32),
            pltpu.VMEM((2, width, width), BF16),
            pltpu.VMEM((2 * width, 16 * width), BF16),
            pltpu.VMEM((RING * width // 2, 16 * width), F32),
            pltpu.VMEM((RING, share, width), F32),
            pltpu.VMEM((2, RING + 2, share, width), F32),
            pltpu.VMEM((STEPS, 2, share // 2, width), F32),
            pltpu.VMEM((STEPS, 2, share // 2, width), F32),
            pltpu.VMEM((STEPS, RING, 16, width), F32),
            pltpu.VMEM((STEPS, RING, 2 * width, width), BF16),
            dma((chunks,)),
            dma((chunks,)),
            dma((2,)),
            dma((2 * STEPS, chunks)),
            dma((2 * STEPS, chunks)),
            dma((2, RING)),
            dma((2, RING)),
            dma((STEPS, 2)),
            dma((STEPS, 2)),
            dma((STEPS, RING)),
            dma((STEPS, RING)),
            pltpu.VMEM((2, 2, share, width), F32),
            dma((2, 2)),
            dma((2, 2)),
            dma((2, 2)),
        ],
        compiler_params=pltpu.CompilerParams(
            collective_id=0, has_side_effects=True, vmem_limit_bytes=50 * 2**20
        ),
        cost_estimate=pl.CostEstimate(
            flops=6 * 9 * 2 * rows * width * width,
            bytes_accessed=4 * rows * width * 4,
            transcendentals=0,
        ),
    )(columns, basis)


def solution(mesh):
    spec = P("factor", "pair")
    return jax.shard_map(
        on_device, mesh=mesh, in_specs=(spec, spec), out_specs=(spec, spec), check_vma=False
    )
```

```python
import functools

import jax
import jax.numpy as jnp
from jax import lax
from jax.experimental import pallas as pl
from jax.experimental.pallas import tpu as pltpu
from jax.sharding import PartitionSpec as P

STEPS = 6
INNER_ROUNDS = 8
MESH = pl.DeviceIdType.MESH
F32 = jnp.float32
BF16 = jnp.bfloat16
WIDTH = 128
HALF = 64
LONG = 1024


def iota(shape, dim):
    return lax.broadcasted_iota(jnp.int32, shape, dim)


def sublane_roll(value, shift):
    return pltpu.roll(value, shift % 8, 0)


def order_of(row, shift):
    inside = lax.rem(row, HALF)
    k = 8 * lax.rem(inside, 8) + inside // 8
    k = jnp.where(row < HALF, k, WIDTH - 1 - k)
    return jnp.where(k == 0, 0, 1 + lax.rem(k - 1 + shift, WIDTH - 1))


def moved_on(first, second):
    top = iota((8, first.shape[1]), 0) == 0
    end = iota((8, first.shape[1]), 0) == 7
    a, b = first, second
    new_first = jnp.concatenate(
        [
            jnp.where(top, a[:8], a[8:16]),
            a[16:],
            jnp.where(end, b[HALF - 8:], sublane_roll(a[:8], -1)),
        ],
        axis=0,
    )
    new_second = jnp.concatenate(
        [jnp.where(top, a[8:16], sublane_roll(b[HALF - 8:], 1)), b[:HALF - 8]], axis=0
    )
    return new_first, new_second


def angles(diag_a, diag_b, cross):
    spread = diag_a - diag_b
    twice = 2.0 * cross
    twice = jnp.where(spread >= 0.0, twice, -twice)
    size = jnp.abs(spread)
    most = jnp.maximum(size, jnp.abs(twice))
    still = most == 0.0
    scale = pl.reciprocal(jnp.where(still, 1.0, most), approx=True)
    size = jnp.where(still, 1.0, size * scale)
    twice = twice * scale
    inverse = lax.rsqrt(size * size + twice * twice)
    cos_sq = 0.5 + 0.5 * size * inverse
    inverse_cos = lax.rsqrt(cos_sq)
    return cos_sq * inverse_cos, 0.5 * twice * inverse * inverse_cos


def lane_sum(value):
    return jnp.broadcast_to(jnp.sum(value, axis=1, keepdims=True), value.shape)


def rotations(gram, start):
    order = start.astype(BF16)
    pieces = [jnp.dot(order, part, preferred_element_type=F32) for part in split(gram, 3)]
    ordered = (pieces[0] + pieces[1]) + pieces[2]
    turn_a, turn_b = start[:HALF], start[HALF:]
    with_a, with_b = ordered[:HALF], ordered[HALF:]
    diag_a, diag_b = lane_sum(turn_a * with_a), lane_sum(turn_b * with_b)
    for round_no in range(INNER_ROUNDS):
        cross = lane_sum(turn_a * with_b)
        cosine, sine = angles(diag_a, diag_b, cross)
        turn_a, turn_b = cosine * turn_a + sine * turn_b, cosine * turn_b - sine * turn_a
        if round_no + 1 < INNER_ROUNDS:
            with_a, with_b = cosine * with_a + sine * with_b, cosine * with_b - sine * with_a
            both = 2.0 * cosine * sine * cross
            cos_sq, sin_sq = cosine * cosine, sine * sine
            diag_a, diag_b = (
                cos_sq * diag_a + sin_sq * diag_b + both,
                cos_sq * diag_b + sin_sq * diag_a - both,
            )
            turn_a, turn_b = moved_on(turn_a, turn_b)
            with_a, with_b = moved_on(with_a, with_b)
            diag_a, diag_b = moved_on(diag_a, diag_b)
    return jnp.concatenate([turn_a, turn_b], axis=0)


def final_order(swapped):
    rows = iota((WIDTH, WIDTH), 0)
    rows = lax.rem(rows + HALF, WIDTH) if swapped else rows
    lanes = iota((WIDTH, WIDTH), 1)
    return jnp.where(order_of(lanes, INNER_ROUNDS - 1) == rows, 1.0, 0.0).astype(BF16)


def in_order(turn, order, parts):
    return [
        jnp.dot(order, part, preferred_element_type=F32).astype(BF16)
        for part in split(turn, parts)
    ]


def swap_halves(value):
    return pltpu.roll(value, HALF, 1)


def split(value, parts):
    out = []
    for _ in range(parts - 1):
        part = value.astype(BF16)
        out.append(part)
        value = value - part.astype(F32)
    out.append(value.astype(BF16))
    return out


def loop(low, high, act):
    def body(at, _):
        act(at)
        return 0

    lax.fori_loop(low, high, body, 0)


def kernel(
    slots, x_in, v_in, x_out, v_out,
    panels, staged, parts_of, gram_sum, turn_parts, start, order,
    load_sem, send_sem, recv_sem,
):
    chunks, _, length = panels.shape[2:]
    me = lax.axis_index("pair")
    factor = lax.axis_index("factor")
    right = lax.rem(me + 1, slots)
    left = lax.rem(me + slots - 1, slots)
    is_first = 1 - (me + slots - 1) // slots
    is_last = (me + 1) // slots

    def rows_of(chunk):
        return pl.ds(pl.multiple_of(chunk * length, length), length)

    def place(step, side):
        return 2 * step + side

    def load(which, chunk):
        return pltpu.make_async_copy(
            (x_in, v_in)[which].at[rows_of(chunk)], staged.at[which, rows_of(chunk)],
            load_sem.at[which, chunk],
        )

    def block(which, step, chunk, side, device):
        at = place(step, side)
        return pltpu.make_async_remote_copy(
            src_ref=panels.at[which, at, chunk],
            dst_ref=panels.at[which, at + 2, chunk],
            send_sem=send_sem.at[which, at, chunk],
            recv_sem=recv_sem.at[which, at, chunk],
            device_id=(factor, device),
            device_id_type=MESH,
        )

    def send_block(which, step, chunk):
        @pl.when(me < slots - 1)
        def _():
            block(which, step, chunk, 0, right).start()

        @pl.when(me > 0)
        def _():
            block(which, step, chunk, 1, left).start()

    def wait_sent(which, step, chunk):
        @pl.when(me < slots - 1)
        def _():
            block(which, step, chunk, 0, right).wait_send()

        @pl.when(me > 0)
        def _():
            block(which, step, chunk, 1, left).wait_send()

    def wait_received(which, step, chunk):
        @pl.when(me > 0)
        def _():
            block(which, step, chunk, 0, right).wait_recv()

        @pl.when(me < slots - 1)
        def _():
            block(which, step, chunk, 1, left).wait_recv()

    for which in range(2):
        loop(0, chunks, lambda chunk: load(which, chunk).start())

    barrier = pltpu.get_barrier_semaphore()
    for neighbour in (left, right):
        pl.semaphore_signal(
            barrier, inc=1, device_id=(factor, neighbour), device_id_type=MESH
        )

    rows = iota((WIDTH, WIDTH), 0)
    lanes = iota((WIDTH, WIDTH), 1)
    start[...] = jnp.where(order_of(rows, 0) == lanes, 1.0, 0.0).astype(F32)
    for swapped in range(2):
        order[swapped] = final_order(swapped)

    def panel(which, step, chunk):
        return jnp.concatenate(
            [panels[which, place(step, 0), chunk], panels[which, place(step, 1), chunk]],
            axis=0,
        )

    def loaded(which, chunk):
        load(which, chunk).wait()
        return staged[which, rows_of(chunk)].T

    def gram(step):
        gram_sum[...] = jnp.zeros_like(gram_sum)

        def add(chunk, value):
            both = jnp.concatenate(split(value, 2), axis=0)
            parts_of[chunk] = both
            gram_sum[...] += lax.dot_general(
                both, both, (((1,), (1,)), ((), ())), preferred_element_type=F32
            )

        def later(chunk):
            wait_received(0, step - 1, chunk)
            add(chunk, panel(0, step, chunk))

        @pl.when(step == 0)
        def _():
            loop(0, chunks, lambda chunk: add(chunk, loaded(0, chunk)))

        pl.when(step > 0)(lambda: loop(0, chunks, later))
        total = gram_sum[...]
        left_sum = total[:WIDTH, :WIDTH] + (total[:WIDTH, WIDTH:] + total[WIDTH:, WIDTH:])
        return left_sum + total[WIDTH:, :WIDTH]

    def give(which, step, chunk, out):
        panels[which, place(step, 0) + 3 * is_last, chunk] = out[:HALF]
        panels[which, place(step, 1) + is_first, chunk] = out[HALF:]
        send_block(which, step, chunk)

    def one_step(step):
        turn = rotations(gram(step), start[...])
        parts = in_order(turn, order[is_first], 3)
        for at, part in enumerate(parts):
            again = part if at < 2 else jnp.zeros_like(part)
            turn_parts[at * WIDTH:(at + 1) * WIDTH] = jnp.concatenate([part, again], axis=1)

        pl.when(step == 0)(lambda: pl.semaphore_wait(barrier, 2))

        def turn_columns(chunk):
            out = jnp.dot(turn_parts[...], parts_of[chunk], preferred_element_type=F32)
            out = out[:WIDTH] + (out[WIDTH:2 * WIDTH] + out[2 * WIDTH:])
            give(0, step, chunk, out)

        loop(0, chunks, turn_columns)

        def turn_basis(chunk, value):
            both = jnp.concatenate(split(value, 2), axis=0)
            out = jnp.dot(turn_parts[:2 * WIDTH], both, preferred_element_type=F32)
            give(1, step, chunk, out[:WIDTH] + out[WIDTH:])

        def later(chunk):
            wait_received(1, step - 1, chunk)
            turn_basis(chunk, panel(1, step, chunk))

        @pl.when(step == 0)
        def _():
            loop(0, chunks, lambda chunk: turn_basis(chunk, loaded(1, chunk)))

        pl.when(step > 0)(lambda: loop(0, chunks, later))

    loop(0, STEPS, one_step)

    for which, target in enumerate((x_out, v_out)):
        def finish(chunk):
            wait_received(which, STEPS - 1, chunk)
            target[rows_of(chunk)] = panel(which, STEPS, chunk).T

        loop(0, chunks, finish)

    def settle(step):
        for which in range(2):
            loop(0, chunks, lambda chunk: wait_sent(which, step, chunk))

    loop(0, STEPS, settle)


def write_out(x, v, x_out, v_out, sem):
    copies = [
        pltpu.make_async_copy(source, target, sem.at[at])
        for at, (source, target) in enumerate(((x, x_out), (v, v_out)))
    ]
    for copy in copies:
        copy.start()
    for copy in copies:
        copy.wait()


def on_device(columns, basis):
    rows, width = columns.shape
    slots = lax.axis_size("pair")
    length = min(LONG, rows)
    chunks = rows // length
    shape = jax.ShapeDtypeStruct((rows, width), F32)
    in_vmem = pltpu.VMEM((rows, width), F32)
    dma = pltpu.SemaphoreType.DMA
    out = pl.pallas_call(
        functools.partial(kernel, slots),
        out_shape=(in_vmem, in_vmem),
        in_specs=[pl.BlockSpec(memory_space=pl.ANY)] * 2,
        out_specs=(pl.BlockSpec(memory_space=pltpu.VMEM),) * 2,
        scratch_shapes=[
            pltpu.VMEM((2, 2 * STEPS + 2, chunks, width // 2, length), F32),
            pltpu.VMEM((2, rows, width), F32),
            pltpu.VMEM((chunks, 2 * width, length), BF16),
            pltpu.VMEM((2 * width, 2 * width), F32),
            pltpu.VMEM((3 * width, 2 * width), BF16),
            pltpu.VMEM((width, width), F32),
            pltpu.VMEM((2, width, width), BF16),
            dma((2, chunks)),
            dma((2, 2 * STEPS, chunks)),
            dma((2, 2 * STEPS, chunks)),
        ],
        compiler_params=pltpu.CompilerParams(
            collective_id=0, has_side_effects=True, vmem_limit_bytes=59 * 2**20
        ),
        cost_estimate=pl.CostEstimate(
            flops=6 * 9 * 2 * rows * width * width,
            bytes_accessed=4 * rows * width * 4,
            transcendentals=0,
        ),
    )(columns, basis)
    return pl.pallas_call(
        write_out,
        out_shape=(shape, shape),
        in_specs=[pl.BlockSpec(memory_space=pltpu.VMEM)] * 2,
        out_specs=(pl.BlockSpec(memory_space=pl.ANY),) * 2,
        scratch_shapes=[dma((2,))],
    )(*out)


def solution(mesh):
    spec = P("factor", "pair")
    return jax.shard_map(
        on_device, mesh=mesh, in_specs=(spec, spec), out_specs=(spec, spec), check_vma=False
    )
```

```python
import functools

import jax
import jax.numpy as jnp
from jax import lax
from jax.experimental import pallas as pl
from jax.experimental.pallas import tpu as pltpu
from jax.sharding import PartitionSpec as P

STEPS = 6
INNER_ROUNDS = 8
MESH = pl.DeviceIdType.MESH
F32 = jnp.float32
BF16 = jnp.bfloat16
WIDTH = 128
HALF = 64
LONG = 1024


def iota(shape, dim):
    return lax.broadcasted_iota(jnp.int32, shape, dim)


def sublane_roll(value, shift):
    return pltpu.roll(value, shift % 8, 0)


def order_of(row, shift):
    inside = lax.rem(row, HALF)
    k = 8 * lax.rem(inside, 8) + inside // 8
    k = jnp.where(row < HALF, k, WIDTH - 1 - k)
    return jnp.where(k == 0, 0, 1 + lax.rem(k - 1 + shift, WIDTH - 1))


def moved_on(first, second):
    top = iota((8, first.shape[1]), 0) == 0
    end = iota((8, first.shape[1]), 0) == 7
    a, b = first, second
    new_first = jnp.concatenate(
        [
            jnp.where(top, a[:8], a[8:16]),
            a[16:],
            jnp.where(end, b[HALF - 8:], sublane_roll(a[:8], -1)),
        ],
        axis=0,
    )
    new_second = jnp.concatenate(
        [jnp.where(top, a[8:16], sublane_roll(b[HALF - 8:], 1)), b[:HALF - 8]], axis=0
    )
    return new_first, new_second


def angles(diag_a, diag_b, cross):
    spread = diag_a - diag_b
    twice = 2.0 * cross
    twice = jnp.where(spread >= 0.0, twice, -twice)
    size = jnp.abs(spread)
    most = jnp.maximum(size, jnp.abs(twice))
    still = most == 0.0
    scale = pl.reciprocal(jnp.where(still, 1.0, most), approx=True)
    size = jnp.where(still, 1.0, size * scale)
    twice = twice * scale
    inverse = lax.rsqrt(size * size + twice * twice)
    cos_sq = 0.5 + 0.5 * size * inverse
    inverse_cos = lax.rsqrt(cos_sq)
    return cos_sq * inverse_cos, 0.5 * twice * inverse * inverse_cos


def lane_sum(value):
    return jnp.broadcast_to(jnp.sum(value, axis=1, keepdims=True), value.shape)


def rotations(gram, start):
    order = start.astype(BF16)
    pieces = [jnp.dot(order, part, preferred_element_type=F32) for part in split(gram, 3)]
    ordered = (pieces[0] + pieces[1]) + pieces[2]
    turn_a, turn_b = start[:HALF], start[HALF:]
    with_a, with_b = ordered[:HALF], ordered[HALF:]
    diag_a, diag_b = lane_sum(turn_a * with_a), lane_sum(turn_b * with_b)
    for round_no in range(INNER_ROUNDS):
        cross = lane_sum(turn_a * with_b)
        cosine, sine = angles(diag_a, diag_b, cross)
        turn_a, turn_b = cosine * turn_a + sine * turn_b, cosine * turn_b - sine * turn_a
        if round_no + 1 < INNER_ROUNDS:
            with_a, with_b = cosine * with_a + sine * with_b, cosine * with_b - sine * with_a
            both = 2.0 * cosine * sine * cross
            cos_sq, sin_sq = cosine * cosine, sine * sine
            diag_a, diag_b = (
                cos_sq * diag_a + sin_sq * diag_b + both,
                cos_sq * diag_b + sin_sq * diag_a - both,
            )
            turn_a, turn_b = moved_on(turn_a, turn_b)
            with_a, with_b = moved_on(with_a, with_b)
            diag_a, diag_b = moved_on(diag_a, diag_b)
    return jnp.concatenate([turn_a, turn_b], axis=0)


def final_order(swapped):
    rows = iota((WIDTH, WIDTH), 0)
    rows = lax.rem(rows + HALF, WIDTH) if swapped else rows
    lanes = iota((WIDTH, WIDTH), 1)
    return jnp.where(order_of(lanes, INNER_ROUNDS - 1) == rows, 1.0, 0.0).astype(BF16)


def in_order(turn, order, parts):
    return [
        jnp.dot(order, part, preferred_element_type=F32).astype(BF16)
        for part in split(turn, parts)
    ]


def swap_halves(value):
    return pltpu.roll(value, HALF, 1)


def split(value, parts):
    out = []
    for _ in range(parts - 1):
        part = value.astype(BF16)
        out.append(part)
        value = value - part.astype(F32)
    out.append(value.astype(BF16))
    return out


def loop(low, high, act):
    def body(at, _):
        act(at)
        return 0

    lax.fori_loop(low, high, body, 0)


def kernel(
    slots, x_in, v_in, x_out, v_out,
    panels, staged, parts_of, gram_sum, turn_parts, start, order,
    load_sem, send_sem, recv_sem,
):
    chunks, _, length = panels.shape[2:]
    me = lax.axis_index("pair")
    factor = lax.axis_index("factor")
    right = lax.rem(me + 1, slots)
    left = lax.rem(me + slots - 1, slots)
    is_first = 1 - (me + slots - 1) // slots
    is_last = (me + 1) // slots

    def rows_of(chunk):
        return pl.ds(pl.multiple_of(chunk * length, length), length)

    def place(step, side):
        return 2 * step + side

    def load(which, chunk):
        return pltpu.make_async_copy(
            (x_in, v_in)[which].at[rows_of(chunk)], staged.at[which, rows_of(chunk)],
            load_sem.at[which, chunk],
        )

    def block(which, step, chunk, side, device):
        at = place(step, side)
        return pltpu.make_async_remote_copy(
            src_ref=panels.at[which, at, chunk],
            dst_ref=panels.at[which, at + 2, chunk],
            send_sem=send_sem.at[which, at, chunk],
            recv_sem=recv_sem.at[which, at, chunk],
            device_id=(factor, device),
            device_id_type=MESH,
        )

    def send_block(which, step, chunk):
        @pl.when(me < slots - 1)
        def _():
            block(which, step, chunk, 0, right).start()

        @pl.when(me > 0)
        def _():
            block(which, step, chunk, 1, left).start()

    def wait_sent(which, step, chunk):
        @pl.when(me < slots - 1)
        def _():
            block(which, step, chunk, 0, right).wait_send()

        @pl.when(me > 0)
        def _():
            block(which, step, chunk, 1, left).wait_send()

    def wait_received(which, step, chunk):
        @pl.when(me > 0)
        def _():
            block(which, step, chunk, 0, right).wait_recv()

        @pl.when(me < slots - 1)
        def _():
            block(which, step, chunk, 1, left).wait_recv()

    for which in range(2):
        loop(0, chunks, lambda chunk: load(which, chunk).start())

    barrier = pltpu.get_barrier_semaphore()
    for neighbour in (left, right):
        pl.semaphore_signal(
            barrier, inc=1, device_id=(factor, neighbour), device_id_type=MESH
        )

    rows = iota((WIDTH, WIDTH), 0)
    lanes = iota((WIDTH, WIDTH), 1)
    start[...] = jnp.where(order_of(rows, 0) == lanes, 1.0, 0.0).astype(F32)
    for swapped in range(2):
        order[swapped] = final_order(swapped)

    def panel(which, step, chunk):
        return jnp.concatenate(
            [panels[which, place(step, 0), chunk], panels[which, place(step, 1), chunk]],
            axis=0,
        )

    def loaded(which, chunk):
        load(which, chunk).wait()
        return staged[which, rows_of(chunk)].T

    def gram(step):
        gram_sum[...] = jnp.zeros_like(gram_sum)

        def add(chunk, value):
            both = jnp.concatenate(split(value, 2), axis=0)
            parts_of[chunk] = both
            gram_sum[...] += lax.dot_general(
                both, both, (((1,), (1,)), ((), ())), preferred_element_type=F32
            )

        def later(chunk):
            wait_received(0, step - 1, chunk)
            add(chunk, panel(0, step, chunk))

        @pl.when(step == 0)
        def _():
            loop(0, chunks, lambda chunk: add(chunk, loaded(0, chunk)))

        pl.when(step > 0)(lambda: loop(0, chunks, later))
        total = gram_sum[...]
        left_sum = total[:WIDTH, :WIDTH] + (total[:WIDTH, WIDTH:] + total[WIDTH:, WIDTH:])
        return left_sum + total[WIDTH:, :WIDTH]

    def give(which, step, chunk, out):
        panels[which, place(step, 0) + 3 * is_last, chunk] = out[:HALF]
        panels[which, place(step, 1) + is_first, chunk] = out[HALF:]
        send_block(which, step, chunk)

    def one_step(step):
        turn = rotations(gram(step), start[...])
        parts = in_order(turn, order[is_first], 3)
        for at, part in enumerate(parts):
            again = part if at < 2 else jnp.zeros_like(part)
            turn_parts[at * WIDTH:(at + 1) * WIDTH] = jnp.concatenate([part, again], axis=1)

        pl.when(step == 0)(lambda: pl.semaphore_wait(barrier, 2))

        def turn_columns(chunk):
            out = jnp.dot(turn_parts[...], parts_of[chunk], preferred_element_type=F32)
            out = out[:WIDTH] + (out[WIDTH:2 * WIDTH] + out[2 * WIDTH:])
            give(0, step, chunk, out)

        loop(0, chunks, turn_columns)

        def turn_basis(chunk, value):
            both = jnp.concatenate(split(value, 2), axis=0)
            out = jnp.dot(turn_parts[:2 * WIDTH], both, preferred_element_type=F32)
            give(1, step, chunk, out[:WIDTH] + out[WIDTH:])

        def later(chunk):
            wait_received(1, step - 1, chunk)
            turn_basis(chunk, panel(1, step, chunk))

        @pl.when(step == 0)
        def _():
            loop(0, chunks, lambda chunk: turn_basis(chunk, loaded(1, chunk)))

        pl.when(step > 0)(lambda: loop(0, chunks, later))

    loop(0, STEPS, one_step)

    for which, target in enumerate((x_out, v_out)):
        def finish(chunk):
            wait_received(which, STEPS - 1, chunk)
            target[rows_of(chunk)] = panel(which, STEPS, chunk).T

        loop(0, chunks, finish)

    def settle(step):
        for which in range(2):
            loop(0, chunks, lambda chunk: wait_sent(which, step, chunk))

    loop(0, STEPS, settle)


def write_out(x, v, x_out, v_out, sem):
    copies = [
        pltpu.make_async_copy(source, target, sem.at[at])
        for at, (source, target) in enumerate(((x, x_out), (v, v_out)))
    ]
    for copy in copies:
        copy.start()
    for copy in copies:
        copy.wait()


def on_device(columns, basis):
    rows, width = columns.shape
    slots = lax.axis_size("pair")
    length = min(LONG, rows)
    chunks = rows // length
    shape = jax.ShapeDtypeStruct((rows, width), F32)
    in_vmem = pltpu.VMEM((rows, width), F32)
    dma = pltpu.SemaphoreType.DMA
    out = pl.pallas_call(
        functools.partial(kernel, slots),
        out_shape=(in_vmem, in_vmem),
        in_specs=[pl.BlockSpec(memory_space=pl.ANY)] * 2,
        out_specs=(pl.BlockSpec(memory_space=pltpu.VMEM),) * 2,
        scratch_shapes=[
            pltpu.VMEM((2, 2 * STEPS + 2, chunks, width // 2, length), F32),
            pltpu.VMEM((2, rows, width), F32),
            pltpu.VMEM((chunks, 2 * width, length), BF16),
            pltpu.VMEM((2 * width, 2 * width), F32),
            pltpu.VMEM((3 * width, 2 * width), BF16),
            pltpu.VMEM((width, width), F32),
            pltpu.VMEM((2, width, width), BF16),
            dma((2, chunks)),
            dma((2, 2 * STEPS, chunks)),
            dma((2, 2 * STEPS, chunks)),
        ],
        compiler_params=pltpu.CompilerParams(
            collective_id=0, has_side_effects=True, vmem_limit_bytes=59 * 2**20
        ),
        cost_estimate=pl.CostEstimate(
            flops=6 * 9 * 2 * rows * width * width,
            bytes_accessed=4 * rows * width * 4,
            transcendentals=0,
        ),
    )(columns, basis)
    return pl.pallas_call(
        write_out,
        out_shape=(shape, shape),
        in_specs=[pl.BlockSpec(memory_space=pl.ANY)] * 2,
        out_specs=(pl.BlockSpec(memory_space=pl.ANY),) * 2,
        scratch_shapes=[dma((2,))],
        compiler_params=pltpu.CompilerParams(vmem_limit_bytes=2**20),
    )(*out)


def solution(mesh):
    spec = P("factor", "pair")
    return jax.shard_map(
        on_device, mesh=mesh, in_specs=(spec, spec), out_specs=(spec, spec), check_vma=False
    )
```

```python
import functools

import jax
import jax.numpy as jnp
from jax import lax
from jax.experimental import pallas as pl
from jax.experimental.pallas import tpu as pltpu
from jax.sharding import PartitionSpec as P

STEPS = 6
INNER_ROUNDS = 8
MESH = pl.DeviceIdType.MESH
F32 = jnp.float32
BF16 = jnp.bfloat16
WIDTH = 128
HALF = 64
LONG = 1024


def iota(shape, dim):
    return lax.broadcasted_iota(jnp.int32, shape, dim)


def sublane_roll(value, shift):
    return pltpu.roll(value, shift % 8, 0)


def order_of(row, shift):
    inside = lax.rem(row, HALF)
    k = 8 * lax.rem(inside, 8) + inside // 8
    k = jnp.where(row < HALF, k, WIDTH - 1 - k)
    return jnp.where(k == 0, 0, 1 + lax.rem(k - 1 + shift, WIDTH - 1))


def moved_on(first, second):
    top = iota((8, first.shape[1]), 0) == 0
    end = iota((8, first.shape[1]), 0) == 7
    a, b = first, second
    new_first = jnp.concatenate(
        [
            jnp.where(top, a[:8], a[8:16]),
            a[16:],
            jnp.where(end, b[HALF - 8:], sublane_roll(a[:8], -1)),
        ],
        axis=0,
    )
    new_second = jnp.concatenate(
        [jnp.where(top, a[8:16], sublane_roll(b[HALF - 8:], 1)), b[:HALF - 8]], axis=0
    )
    return new_first, new_second


def angles(diag_a, diag_b, cross):
    spread = diag_a - diag_b
    twice = 2.0 * cross
    twice = jnp.where(spread >= 0.0, twice, -twice)
    size = jnp.abs(spread)
    most = jnp.maximum(size, jnp.abs(twice))
    still = most == 0.0
    scale = pl.reciprocal(jnp.where(still, 1.0, most), approx=True)
    size = jnp.where(still, 1.0, size * scale)
    twice = twice * scale
    inverse = lax.rsqrt(size * size + twice * twice)
    cos_sq = 0.5 + 0.5 * size * inverse
    inverse_cos = lax.rsqrt(cos_sq)
    return cos_sq * inverse_cos, 0.5 * twice * inverse * inverse_cos


def lane_sum(value):
    return jnp.broadcast_to(jnp.sum(value, axis=1, keepdims=True), value.shape)


def rotations(gram, start):
    order = start.astype(BF16)
    pieces = [jnp.dot(order, part, preferred_element_type=F32) for part in split(gram, 3)]
    ordered = (pieces[0] + pieces[1]) + pieces[2]
    turn_a, turn_b = start[:HALF], start[HALF:]
    with_a, with_b = ordered[:HALF], ordered[HALF:]
    diag_a, diag_b = lane_sum(turn_a * with_a), lane_sum(turn_b * with_b)
    for round_no in range(INNER_ROUNDS):
        cross = lane_sum(turn_a * with_b)
        cosine, sine = angles(diag_a, diag_b, cross)
        turn_a, turn_b = cosine * turn_a + sine * turn_b, cosine * turn_b - sine * turn_a
        if round_no + 1 < INNER_ROUNDS:
            with_a, with_b = cosine * with_a + sine * with_b, cosine * with_b - sine * with_a
            both = 2.0 * cosine * sine * cross
            cos_sq, sin_sq = cosine * cosine, sine * sine
            diag_a, diag_b = (
                cos_sq * diag_a + sin_sq * diag_b + both,
                cos_sq * diag_b + sin_sq * diag_a - both,
            )
            turn_a, turn_b = moved_on(turn_a, turn_b)
            with_a, with_b = moved_on(with_a, with_b)
            diag_a, diag_b = moved_on(diag_a, diag_b)
    return jnp.concatenate([turn_a, turn_b], axis=0)


def final_order(swapped):
    rows = iota((WIDTH, WIDTH), 0)
    rows = lax.rem(rows + HALF, WIDTH) if swapped else rows
    lanes = iota((WIDTH, WIDTH), 1)
    return jnp.where(order_of(lanes, INNER_ROUNDS - 1) == rows, 1.0, 0.0).astype(BF16)


def in_order(turn, order, parts):
    return [
        jnp.dot(order, part, preferred_element_type=F32).astype(BF16)
        for part in split(turn, parts)
    ]


def swap_halves(value):
    return pltpu.roll(value, HALF, 1)


def split(value, parts):
    out = []
    for _ in range(parts - 1):
        part = value.astype(BF16)
        out.append(part)
        value = value - part.astype(F32)
    out.append(value.astype(BF16))
    return out


def loop(low, high, act):
    def body(at, _):
        act(at)
        return 0

    lax.fori_loop(low, high, body, 0)


def kernel(
    slots, x_in, v_in, x_out, v_out,
    panels, staged, parts_of, gram_sum, turn_parts, start, order, raw, turn_give, turn_take,
    load_sem, send_sem, recv_sem, raw_send, raw_recv, turn_send, turn_recv,
):
    chunks, _, length = panels.shape[2:]
    me = lax.axis_index("pair")
    factor = lax.axis_index("factor")
    right = lax.rem(me + 1, slots)
    left = lax.rem(me + slots - 1, slots)
    is_first = 1 - (me + slots - 1) // slots
    is_last = (me + 1) // slots

    def rows_of(chunk):
        return pl.ds(pl.multiple_of(chunk * length, length), length)

    def place(step, side):
        return 2 * step + side

    def load(which, chunk):
        return pltpu.make_async_copy(
            (x_in, v_in)[which].at[rows_of(chunk)], staged.at[which, rows_of(chunk)],
            load_sem.at[which, chunk],
        )

    def block(which, step, chunk, side, device):
        at = place(step, side)
        return pltpu.make_async_remote_copy(
            src_ref=panels.at[which, at, chunk],
            dst_ref=panels.at[which, at + 2, chunk],
            send_sem=send_sem.at[which, at, chunk],
            recv_sem=recv_sem.at[which, at, chunk],
            device_id=(factor, device),
            device_id_type=MESH,
        )

    def remote(src, dst, send, recv, device):
        return pltpu.make_async_remote_copy(
            src_ref=src, dst_ref=dst, send_sem=send, recv_sem=recv,
            device_id=(factor, device), device_id_type=MESH,
        )

    def as_came(side):
        return remote(
            v_in.at[rows_of(0)], raw.at[side], raw_send.at[side], raw_recv.at[side],
            (right, left)[side],
        )

    def turn_rows(side):
        return remote(
            turn_give.at[side], turn_take.at[side], turn_send.at[side], turn_recv.at[side],
            (right, left)[side],
        )

    gives = (me < slots - 1, me > 0)
    takes = (me > 0, me < slots - 1)

    def send_block(which, step, chunk):
        @pl.when(me < slots - 1)
        def _():
            block(which, step, chunk, 0, right).start()

        @pl.when(me > 0)
        def _():
            block(which, step, chunk, 1, left).start()

    def wait_sent(which, step, chunk):
        @pl.when(me < slots - 1)
        def _():
            block(which, step, chunk, 0, right).wait_send()

        @pl.when(me > 0)
        def _():
            block(which, step, chunk, 1, left).wait_send()

    def wait_received(which, step, chunk):
        @pl.when(me > 0)
        def _():
            block(which, step, chunk, 0, right).wait_recv()

        @pl.when(me < slots - 1)
        def _():
            block(which, step, chunk, 1, left).wait_recv()

    for which in range(2):
        loop(0, chunks, lambda chunk: load(which, chunk).start())

    barrier = pltpu.get_barrier_semaphore()
    for neighbour in (left, right):
        pl.semaphore_signal(
            barrier, inc=1, device_id=(factor, neighbour), device_id_type=MESH
        )
    pl.semaphore_wait(barrier, 2)
    for side in range(2):
        pl.when(gives[side])(lambda: as_came(side).start())

    rows = iota((WIDTH, WIDTH), 0)
    lanes = iota((WIDTH, WIDTH), 1)
    start[...] = jnp.where(order_of(rows, 0) == lanes, 1.0, 0.0).astype(F32)
    for swapped in range(2):
        order[swapped] = final_order(swapped)

    def panel(which, step, chunk):
        return jnp.concatenate(
            [panels[which, place(step, 0), chunk], panels[which, place(step, 1), chunk]],
            axis=0,
        )

    def loaded(which, chunk):
        load(which, chunk).wait()
        return staged[which, rows_of(chunk)].T

    def gram(step):
        gram_sum[...] = jnp.zeros_like(gram_sum)

        def add(chunk, value):
            both = jnp.concatenate(split(value, 2), axis=0)
            parts_of[chunk] = both
            gram_sum[...] += lax.dot_general(
                both, both, (((1,), (1,)), ((), ())), preferred_element_type=F32
            )

        def later(chunk):
            wait_received(0, step - 1, chunk)
            add(chunk, panel(0, step, chunk))

        @pl.when(step == 0)
        def _():
            loop(0, chunks, lambda chunk: add(chunk, loaded(0, chunk)))

        pl.when(step > 0)(lambda: loop(0, chunks, later))
        total = gram_sum[...]
        left_sum = total[:WIDTH, :WIDTH] + (total[:WIDTH, WIDTH:] + total[WIDTH:, WIDTH:])
        return left_sum + total[WIDTH:, :WIDTH]

    def give(which, step, chunk, out):
        panels[which, place(step, 0) + 3 * is_last, chunk] = out[:HALF]
        panels[which, place(step, 1) + is_first, chunk] = out[HALF:]
        send_block(which, step, chunk)

    def turn_neighbour(side):
        @pl.when(takes[side])
        def _():
            as_came(side).wait_recv()
            turn_rows(side).wait_recv()

        @pl.when(jnp.logical_not(takes[side]))
        def _():
            raw[side] = staged[1, rows_of(0)]
            turn_take[side] = turn_give[1 - side]

        high, low = split(turn_take[side], 2)
        lhs = jnp.concatenate([high, low], axis=0)
        both = jnp.concatenate(split(raw[side].T, 2), axis=0)
        out = jnp.dot(
            jnp.concatenate([lhs, lhs], axis=1), both, preferred_element_type=F32
        )
        panels[1, place(1, side), 0] = out[:HALF] + out[HALF:]

    def one_step(step):
        turn = rotations(gram(step), start[...])
        parts = in_order(turn, order[is_first], 3)
        for at, part in enumerate(parts):
            again = part if at < 2 else jnp.zeros_like(part)
            turn_parts[at * WIDTH:(at + 1) * WIDTH] = jnp.concatenate([part, again], axis=1)

        def turn_columns(chunk):
            out = jnp.dot(turn_parts[...], parts_of[chunk], preferred_element_type=F32)
            out = out[:WIDTH] + (out[WIDTH:2 * WIDTH] + out[2 * WIDTH:])
            give(0, step, chunk, out)

        loop(0, chunks, turn_columns)

        def turn_basis(chunk, value):
            both = jnp.concatenate(split(value, 2), axis=0)
            out = jnp.dot(turn_parts[:2 * WIDTH], both, preferred_element_type=F32)
            give(1, step, chunk, out[:WIDTH] + out[WIDTH:])

        def later(chunk):
            pl.when((step > 1) | (chunk > 0))(lambda: wait_received(1, step - 1, chunk))
            turn_basis(chunk, panel(1, step, chunk))

        @pl.when(step == 0)
        def _():
            for side in range(2):
                high, low = (
                    turn_parts[at:at + HALF, :WIDTH].astype(F32)
                    for at in (side * HALF, WIDTH + side * HALF)
                )
                turn_give[side] = high + low
                pl.when(gives[side])(lambda: turn_rows(side).start())
            loop(1, chunks, lambda chunk: turn_basis(chunk, loaded(1, chunk)))
            load(1, 0).wait()
            for side in range(2):
                turn_neighbour(side)

        pl.when(step > 0)(lambda: loop(0, chunks, later))

    loop(0, STEPS, one_step)

    for which, target in enumerate((x_out, v_out)):
        def finish(chunk):
            wait_received(which, STEPS - 1, chunk)
            target[rows_of(chunk)] = panel(which, STEPS, chunk).T

        loop(0, chunks, finish)

    def settle(step):
        loop(0, chunks, lambda chunk: wait_sent(0, step, chunk))
        none = 1 - (step + STEPS - 1) // STEPS
        loop(none, chunks, lambda chunk: wait_sent(1, step, chunk))

    loop(0, STEPS, settle)
    for side in range(2):
        pl.when(gives[side])(lambda: as_came(side).wait_send())
        pl.when(gives[side])(lambda: turn_rows(side).wait_send())


def write_out(x, v, x_out, v_out, sem):
    length = x.shape[0] // sem.shape[1]
    copies = []
    for chunk in range(sem.shape[1]):
        at = pl.ds(chunk * length, length)
        for which, (source, target) in enumerate(((x, x_out), (v, v_out))):
            copies.append(
                pltpu.make_async_copy(source.at[at], target.at[at], sem.at[which, chunk])
            )
    for copy in copies:
        copy.start()
    for copy in copies:
        copy.wait()


def on_device(columns, basis):
    rows, width = columns.shape
    slots = lax.axis_size("pair")
    length = min(LONG, rows)
    chunks = rows // length
    shape = jax.ShapeDtypeStruct((rows, width), F32)
    in_vmem = pltpu.VMEM((rows, width), F32)
    dma = pltpu.SemaphoreType.DMA
    out = pl.pallas_call(
        functools.partial(kernel, slots),
        out_shape=(in_vmem, in_vmem),
        in_specs=[pl.BlockSpec(memory_space=pl.ANY)] * 2,
        out_specs=(pl.BlockSpec(memory_space=pltpu.VMEM),) * 2,
        scratch_shapes=[
            pltpu.VMEM((2, 2 * STEPS + 2, chunks, width // 2, length), F32),
            pltpu.VMEM((2, rows, width), F32),
            pltpu.VMEM((chunks, 2 * width, length), BF16),
            pltpu.VMEM((2 * width, 2 * width), F32),
            pltpu.VMEM((3 * width, 2 * width), BF16),
            pltpu.VMEM((width, width), F32),
            pltpu.VMEM((2, width, width), BF16),
            pltpu.VMEM((2, length, width), F32),
            pltpu.VMEM((2, width // 2, width), F32),
            pltpu.VMEM((2, width // 2, width), F32),
            dma((2, chunks)),
            dma((2, 2 * STEPS, chunks)),
            dma((2, 2 * STEPS, chunks)),
            dma((2,)),
            dma((2,)),
            dma((2,)),
            dma((2,)),
        ],
        compiler_params=pltpu.CompilerParams(
            collective_id=0, has_side_effects=True, vmem_limit_bytes=59 * 2**20
        ),
        cost_estimate=pl.CostEstimate(
            flops=6 * 9 * 2 * rows * width * width,
            bytes_accessed=4 * rows * width * 4,
            transcendentals=0,
        ),
    )(columns, basis)
    return pl.pallas_call(
        write_out,
        out_shape=(shape, shape),
        in_specs=[pl.BlockSpec(memory_space=pl.ANY)] * 2,
        out_specs=(pl.BlockSpec(memory_space=pl.ANY),) * 2,
        scratch_shapes=[dma((2, 4))],
        compiler_params=pltpu.CompilerParams(vmem_limit_bytes=2**20),
    )(*out)


def solution(mesh):
    spec = P("factor", "pair")
    return jax.shard_map(
        on_device, mesh=mesh, in_specs=(spec, spec), out_specs=(spec, spec), check_vma=False
    )
```

```python
import functools

import jax
import jax.numpy as jnp
from jax import lax
from jax.experimental import pallas as pl
from jax.experimental.pallas import tpu as pltpu
from jax.sharding import PartitionSpec as P

STEPS = 6
INNER_ROUNDS = 8
MESH = pl.DeviceIdType.MESH
F32 = jnp.float32
BF16 = jnp.bfloat16
WIDTH = 128
HALF = 64
LONG = 1024


def iota(shape, dim):
    return lax.broadcasted_iota(jnp.int32, shape, dim)


def sublane_roll(value, shift):
    return pltpu.roll(value, shift % 8, 0)


def order_of(row, shift):
    inside = lax.rem(row, HALF)
    k = 8 * lax.rem(inside, 8) + inside // 8
    k = jnp.where(row < HALF, k, WIDTH - 1 - k)
    return jnp.where(k == 0, 0, 1 + lax.rem(k - 1 + shift, WIDTH - 1))


def moved_on(first, second):
    top = iota((8, first.shape[1]), 0) == 0
    end = iota((8, first.shape[1]), 0) == 7
    a, b = first, second
    new_first = jnp.concatenate(
        [
            jnp.where(top, a[:8], a[8:16]),
            a[16:],
            jnp.where(end, b[HALF - 8:], sublane_roll(a[:8], -1)),
        ],
        axis=0,
    )
    new_second = jnp.concatenate(
        [jnp.where(top, a[8:16], sublane_roll(b[HALF - 8:], 1)), b[:HALF - 8]], axis=0
    )
    return new_first, new_second


def angles(diag_a, diag_b, cross):
    spread = diag_a - diag_b
    twice = 2.0 * cross
    twice = jnp.where(spread >= 0.0, twice, -twice)
    size = jnp.abs(spread)
    most = jnp.maximum(size, jnp.abs(twice))
    still = most == 0.0
    scale = pl.reciprocal(jnp.where(still, 1.0, most), approx=True)
    size = jnp.where(still, 1.0, size * scale)
    twice = twice * scale
    inverse = lax.rsqrt(size * size + twice * twice)
    cos_sq = 0.5 + 0.5 * size * inverse
    inverse_cos = lax.rsqrt(cos_sq)
    return cos_sq * inverse_cos, 0.5 * twice * inverse * inverse_cos


def lane_sum(value):
    return jnp.broadcast_to(jnp.sum(value, axis=1, keepdims=True), value.shape)


def rotations(gram, start):
    order = start.astype(BF16)
    pieces = [jnp.dot(order, part, preferred_element_type=F32) for part in split(gram, 3)]
    ordered = (pieces[0] + pieces[1]) + pieces[2]
    turn_a, turn_b = start[:HALF], start[HALF:]
    with_a, with_b = ordered[:HALF], ordered[HALF:]
    diag_a, diag_b = lane_sum(turn_a * with_a), lane_sum(turn_b * with_b)
    for round_no in range(INNER_ROUNDS):
        cross = lane_sum(turn_a * with_b)
        cosine, sine = angles(diag_a, diag_b, cross)
        turn_a, turn_b = cosine * turn_a + sine * turn_b, cosine * turn_b - sine * turn_a
        if round_no + 1 < INNER_ROUNDS:
            with_a, with_b = cosine * with_a + sine * with_b, cosine * with_b - sine * with_a
            both = 2.0 * cosine * sine * cross
            cos_sq, sin_sq = cosine * cosine, sine * sine
            diag_a, diag_b = (
                cos_sq * diag_a + sin_sq * diag_b + both,
                cos_sq * diag_b + sin_sq * diag_a - both,
            )
            turn_a, turn_b = moved_on(turn_a, turn_b)
            with_a, with_b = moved_on(with_a, with_b)
            diag_a, diag_b = moved_on(diag_a, diag_b)
    return jnp.concatenate([turn_a, turn_b], axis=0)


def final_order(swapped):
    rows = iota((WIDTH, WIDTH), 0)
    rows = lax.rem(rows + HALF, WIDTH) if swapped else rows
    lanes = iota((WIDTH, WIDTH), 1)
    return jnp.where(order_of(lanes, INNER_ROUNDS - 1) == rows, 1.0, 0.0).astype(BF16)


def in_order(turn, order, parts):
    return [
        jnp.dot(order, part, preferred_element_type=F32).astype(BF16)
        for part in split(turn, parts)
    ]


def swap_halves(value):
    return pltpu.roll(value, HALF, 1)


def split(value, parts):
    out = []
    for _ in range(parts - 1):
        part = value.astype(BF16)
        out.append(part)
        value = value - part.astype(F32)
    out.append(value.astype(BF16))
    return out


def loop(low, high, act):
    def body(at, _):
        act(at)
        return 0

    lax.fori_loop(low, high, body, 0)


def kernel(
    slots, x_in, v_in, x_out, v_out,
    panels, staged, parts_of, gram_sum, turn_parts, start, order, raw, turn_give, turn_take,
    load_sem, send_sem, recv_sem, raw_send, raw_recv, turn_send, turn_recv,
):
    chunks, _, length = panels.shape[2:]
    me = lax.axis_index("pair")
    factor = lax.axis_index("factor")
    right = lax.rem(me + 1, slots)
    left = lax.rem(me + slots - 1, slots)
    is_first = 1 - (me + slots - 1) // slots
    is_last = (me + 1) // slots

    def rows_of(chunk):
        return pl.ds(pl.multiple_of(chunk * length, length), length)

    def place(step, side):
        return 2 * step + side

    def load(which, chunk):
        return pltpu.make_async_copy(
            (x_in, v_in)[which].at[rows_of(chunk)], staged.at[which, rows_of(chunk)],
            load_sem.at[which, chunk],
        )

    def block(which, step, chunk, side, device):
        at = place(step, side)
        return pltpu.make_async_remote_copy(
            src_ref=panels.at[which, at, chunk],
            dst_ref=panels.at[which, at + 2, chunk],
            send_sem=send_sem.at[which, at, chunk],
            recv_sem=recv_sem.at[which, at, chunk],
            device_id=(factor, device),
            device_id_type=MESH,
        )

    def remote(src, dst, send, recv, device):
        return pltpu.make_async_remote_copy(
            src_ref=src, dst_ref=dst, send_sem=send, recv_sem=recv,
            device_id=(factor, device), device_id_type=MESH,
        )

    def as_came(side):
        return remote(
            v_in.at[rows_of(0)], raw.at[side], raw_send.at[side], raw_recv.at[side],
            (right, left)[side],
        )

    def turn_rows(side):
        return remote(
            turn_give.at[side], turn_take.at[side], turn_send.at[side], turn_recv.at[side],
            (right, left)[side],
        )

    gives = (me < slots - 1, me > 0)
    takes = (me > 0, me < slots - 1)

    def send_block(which, step, chunk):
        @pl.when(me < slots - 1)
        def _():
            block(which, step, chunk, 0, right).start()

        @pl.when(me > 0)
        def _():
            block(which, step, chunk, 1, left).start()

    def wait_sent(which, step, chunk):
        @pl.when(me < slots - 1)
        def _():
            block(which, step, chunk, 0, right).wait_send()

        @pl.when(me > 0)
        def _():
            block(which, step, chunk, 1, left).wait_send()

    def wait_received(which, step, chunk):
        @pl.when(me > 0)
        def _():
            block(which, step, chunk, 0, right).wait_recv()

        @pl.when(me < slots - 1)
        def _():
            block(which, step, chunk, 1, left).wait_recv()

    for which in range(2):
        loop(0, chunks, lambda chunk: load(which, chunk).start())

    barrier = pltpu.get_barrier_semaphore()
    for neighbour in (left, right):
        pl.semaphore_signal(
            barrier, inc=1, device_id=(factor, neighbour), device_id_type=MESH
        )
    pl.semaphore_wait(barrier, 2)
    for side in range(2):
        pl.when(gives[side])(lambda: as_came(side).start())

    rows = iota((WIDTH, WIDTH), 0)
    lanes = iota((WIDTH, WIDTH), 1)
    start[...] = jnp.where(order_of(rows, 0) == lanes, 1.0, 0.0).astype(F32)
    for swapped in range(2):
        order[swapped] = final_order(swapped)

    def panel(which, step, chunk):
        return jnp.concatenate(
            [panels[which, place(step, 0), chunk], panels[which, place(step, 1), chunk]],
            axis=0,
        )

    def loaded(which, chunk):
        load(which, chunk).wait()
        return staged[which, rows_of(chunk)].T

    def gram(step):
        gram_sum[...] = jnp.zeros_like(gram_sum)

        def add(chunk, value):
            both = jnp.concatenate(split(value, 2), axis=0)
            parts_of[chunk] = both
            gram_sum[...] += lax.dot_general(
                both, both, (((1,), (1,)), ((), ())), preferred_element_type=F32
            )

        def later(chunk):
            wait_received(0, step - 1, chunk)
            add(chunk, panel(0, step, chunk))

        @pl.when(step == 0)
        def _():
            loop(0, chunks, lambda chunk: add(chunk, loaded(0, chunk)))

        pl.when(step > 0)(lambda: loop(0, chunks, later))
        total = gram_sum[...]
        left_sum = total[:WIDTH, :WIDTH] + (total[:WIDTH, WIDTH:] + total[WIDTH:, WIDTH:])
        return left_sum + total[WIDTH:, :WIDTH]

    def give(which, step, chunk, out):
        panels[which, place(step, 0) + 3 * is_last, chunk] = out[:HALF]
        panels[which, place(step, 1) + is_first, chunk] = out[HALF:]
        send_block(which, step, chunk)

    def turn_neighbour(side):
        @pl.when(takes[side])
        def _():
            as_came(side).wait_recv()
            turn_rows(side).wait_recv()

        @pl.when(jnp.logical_not(takes[side]))
        def _():
            raw[side] = staged[1, rows_of(0)]
            turn_take[side] = turn_give[1 - side]

        high, low = split(turn_take[side], 2)
        lhs = jnp.concatenate([high, low], axis=0)
        both = jnp.concatenate(split(raw[side].T, 2), axis=0)
        out = jnp.dot(
            jnp.concatenate([lhs, lhs], axis=1), both, preferred_element_type=F32
        )
        panels[1, place(1, side), 0] = out[:HALF] + out[HALF:]

    def one_step(step):
        turn = rotations(gram(step), start[...])
        parts = in_order(turn, order[is_first], 3)
        for at, part in enumerate(parts):
            again = part if at < 2 else jnp.zeros_like(part)
            turn_parts[at * WIDTH:(at + 1) * WIDTH] = jnp.concatenate([part, again], axis=1)

        def turn_columns(chunk):
            out = jnp.dot(turn_parts[...], parts_of[chunk], preferred_element_type=F32)
            out = out[:WIDTH] + (out[WIDTH:2 * WIDTH] + out[2 * WIDTH:])
            give(0, step, chunk, out)

        loop(0, chunks, turn_columns)

        def turn_basis(chunk, value):
            both = jnp.concatenate(split(value, 2), axis=0)
            out = jnp.dot(turn_parts[:2 * WIDTH], both, preferred_element_type=F32)
            give(1, step, chunk, out[:WIDTH] + out[WIDTH:])

        def later(chunk):
            pl.when((step > 1) | (chunk > 0))(lambda: wait_received(1, step - 1, chunk))
            turn_basis(chunk, panel(1, step, chunk))

        @pl.when(step == 0)
        def _():
            for side in range(2):
                high, low = (
                    turn_parts[at:at + HALF, :WIDTH].astype(F32)
                    for at in (side * HALF, WIDTH + side * HALF)
                )
                turn_give[side] = high + low
                pl.when(gives[side])(lambda: turn_rows(side).start())
            loop(1, chunks, lambda chunk: turn_basis(chunk, loaded(1, chunk)))

        @pl.when(step == 1)
        def _():
            load(1, 0).wait()
            for side in range(2):
                turn_neighbour(side)

        pl.when(step > 0)(lambda: loop(0, chunks, later))

    loop(0, STEPS, one_step)

    for which, target in enumerate((x_out, v_out)):
        def finish(chunk):
            wait_received(which, STEPS - 1, chunk)
            target[rows_of(chunk)] = panel(which, STEPS, chunk).T

        loop(0, chunks, finish)

    def settle(step):
        loop(0, chunks, lambda chunk: wait_sent(0, step, chunk))
        none = 1 - (step + STEPS - 1) // STEPS
        loop(none, chunks, lambda chunk: wait_sent(1, step, chunk))

    loop(0, STEPS, settle)
    for side in range(2):
        pl.when(gives[side])(lambda: as_came(side).wait_send())
        pl.when(gives[side])(lambda: turn_rows(side).wait_send())


def write_out(x, v, x_out, v_out, sem):
    length = x.shape[0] // sem.shape[1]
    copies = []
    for chunk in range(sem.shape[1]):
        at = pl.ds(chunk * length, length)
        for which, (source, target) in enumerate(((x, x_out), (v, v_out))):
            copies.append(
                pltpu.make_async_copy(source.at[at], target.at[at], sem.at[which, chunk])
            )
    for copy in copies:
        copy.start()
    for copy in copies:
        copy.wait()


def on_device(columns, basis):
    rows, width = columns.shape
    slots = lax.axis_size("pair")
    length = min(LONG, rows)
    chunks = rows // length
    shape = jax.ShapeDtypeStruct((rows, width), F32)
    in_vmem = pltpu.VMEM((rows, width), F32)
    dma = pltpu.SemaphoreType.DMA
    out = pl.pallas_call(
        functools.partial(kernel, slots),
        out_shape=(in_vmem, in_vmem),
        in_specs=[pl.BlockSpec(memory_space=pl.ANY)] * 2,
        out_specs=(pl.BlockSpec(memory_space=pltpu.VMEM),) * 2,
        scratch_shapes=[
            pltpu.VMEM((2, 2 * STEPS + 2, chunks, width // 2, length), F32),
            pltpu.VMEM((2, rows, width), F32),
            pltpu.VMEM((chunks, 2 * width, length), BF16),
            pltpu.VMEM((2 * width, 2 * width), F32),
            pltpu.VMEM((3 * width, 2 * width), BF16),
            pltpu.VMEM((width, width), F32),
            pltpu.VMEM((2, width, width), BF16),
            pltpu.VMEM((2, length, width), F32),
            pltpu.VMEM((2, width // 2, width), F32),
            pltpu.VMEM((2, width // 2, width), F32),
            dma((2, chunks)),
            dma((2, 2 * STEPS, chunks)),
            dma((2, 2 * STEPS, chunks)),
            dma((2,)),
            dma((2,)),
            dma((2,)),
            dma((2,)),
        ],
        compiler_params=pltpu.CompilerParams(
            collective_id=0, has_side_effects=True, vmem_limit_bytes=59 * 2**20
        ),
        cost_estimate=pl.CostEstimate(
            flops=6 * 9 * 2 * rows * width * width,
            bytes_accessed=4 * rows * width * 4,
            transcendentals=0,
        ),
    )(columns, basis)
    return pl.pallas_call(
        write_out,
        out_shape=(shape, shape),
        in_specs=[pl.BlockSpec(memory_space=pl.ANY)] * 2,
        out_specs=(pl.BlockSpec(memory_space=pl.ANY),) * 2,
        scratch_shapes=[dma((2, 4))],
        compiler_params=pltpu.CompilerParams(vmem_limit_bytes=2**20),
    )(*out)


def solution(mesh):
    spec = P("factor", "pair")
    return jax.shard_map(
        on_device, mesh=mesh, in_specs=(spec, spec), out_specs=(spec, spec), check_vma=False
    )
```
